512 devices in a mesh: dp: 8 (over z_lo), tm: 4 (over z_hi, core), space: 16 (over y, x).
Axes of the slice: x: 4, y: 4, z: 16 (z_hi: 2, z_lo: 8; z = z_hi * 8 + z_lo), core: 2. Of those that a mesh axis runs over, the one named last changes fastest.
Arguments:
- patches: bfloat16 [8, 8, 1024, 1152], P('dp', 'tm', 'space'), may hold values from -4 to 4
- query_s: bfloat16 [8, 8, 1024, 1152], P('dp', 'tm', 'space'), may hold values from -8 to 8
- key_s: bfloat16 [8, 8, 1024, 1152], P('dp', 'tm', 'space'), may hold values from -8 to 8
- value_s: bfloat16 [8, 8, 1024, 1152], P('dp', 'tm', 'space'), may hold values from -6 to 6
- query_t: bfloat16 [8, 8, 1024, 1152], P('dp', 'tm', 'space'), may hold values from -8 to 8
- key_t: bfloat16 [8, 8, 1024, 1152], P('dp', 'tm', 'space'), may hold values from -8 to 8
- value_t: bfloat16 [8, 8, 1024, 1152], P('dp', 'tm', 'space'), may hold values from -6 to 6
- adapters_a: bfloat16 [4, 1152, 16], replicated, may hold values from -0.1875 to 0.1875
- adapters_b: bfloat16 [4, 16, 1152], replicated, may hold values from -1.5 to 1.5
- cotangent: bfloat16 [8, 8, 1024, 1152], P('dp', 'tm', 'space'), may hold values from -6 to 6
Outputs:
- mixed: bfloat16 [8, 8, 1024, 1152], P('dp', 'tm', 'space')
- grads_a: float32 [4, 1152, 16], replicated
- grads_b: float32 [4, 16, 1152], replicated
The draws below stay inside these ranges and needn't reach their ends.
All inputs are finite; a program needn't handle non-finite values.
Results may differ from the reference program's by a relative error of at most 0.018.
The reference program's roundings to bfloat16 on the way (of `probs_low`, `o_s`, `hidden`, `o_t`, `dscore` and `dhidden`) count: a program that leaves them out, or rounds other values in their place, can miss the bound.
Values may be sent and summed in bfloat16 or wider, within the bound.
A program may use at most 64 MiB of HBM per device.

```python
import jax
import jax.numpy as jnp
from jax import lax

D = 1152
HEADS = 16
RANK = 16
HEAD_DIM = 72
CLIPS = 8
FRAMES = 8
PATCHES = 1024


def paired(key):
    shape = (CLIPS, FRAMES, PATCHES, D)
    first, second = jax.random.split(key, 2)
    keys = 1.4 * jnp.clip(jax.random.normal(first, shape, jnp.float32), -4.0, 4.0)
    query = 1.4 * jnp.clip(jax.random.normal(second, shape, jnp.float32), -4.0, 4.0)
    return (query.astype(jnp.bfloat16), keys.astype(jnp.bfloat16))


def draw_query_s(key, part):
    return paired(jax.random.fold_in(key, 11))[0]


def draw_key_s(key, part):
    return paired(jax.random.fold_in(key, 11))[1]


def draw_query_t(key, part):
    return paired(jax.random.fold_in(key, 12))[0]


def draw_key_t(key, part):
    return paired(jax.random.fold_in(key, 12))[1]


def shard_levels(own_key, dims, cuts, least, high):
    def one(dim, shards_of):
        draws = jax.random.uniform(jax.random.fold_in(jax.random.fold_in(own_key, 6), dim), (shards_of,), jnp.float32, least / len(cuts), high / len(cuts))
        return jnp.repeat(jnp.exp(draws), dims[dim] // shards_of).reshape((-1,) + (1,) * (len(dims) - dim - 1))

    factor_of = one(*cuts[0])
    for cut in cuts[1:]:
        factor_of = factor_of * one(*cut)
    return factor_of


def normal_values(rng, extent, width, reach, cuts=(), kind=jnp.bfloat16):
    level = shard_levels(rng, extent, cuts, -0.22, 0.18) if cuts else 1.0
    drawn = jax.random.normal(rng, extent, jnp.float32) * width * level
    return jnp.minimum(jnp.maximum(drawn, -reach), reach).astype(kind)


def setup_inputs(seed: int = 0) -> dict:
    key_of = jax.random.split(jax.random.key(seed), 11)
    return {
        "patches": normal_values(key_of[0], (CLIPS, FRAMES, PATCHES, D), 0.5, 4.0, ((0, 8), (1, 4), (2, 16))),
        "query_s": draw_query_s(jax.random.fold_in(key_of[10], 71), 0),
        "key_s": draw_key_s(jax.random.fold_in(key_of[10], 71), 0),
        "value_s": normal_values(key_of[3], (CLIPS, FRAMES, PATCHES, D), 1.0, 6.0, ((0, 8), (1, 4), (2, 16))),
        "query_t": draw_query_t(jax.random.fold_in(key_of[10], 71), 0),
        "key_t": draw_key_t(jax.random.fold_in(key_of[10], 71), 0),
        "value_t": normal_values(key_of[6], (CLIPS, FRAMES, PATCHES, D), 1.0, 6.0, ((0, 8), (1, 4), (2, 16))),
        "adapters_a": normal_values(key_of[7], (4, D, RANK), D ** -0.5, 0.1875),
        "adapters_b": normal_values(key_of[8], (4, RANK, D), RANK ** -0.5, 1.5),
        "cotangent": normal_values(key_of[9], (CLIPS, FRAMES, PATCHES, D), 1.0, 6.0, ((0, 8), (1, 4), (2, 16))),
    }


def softmax_probs(query, keys):
    length = query.shape[0]
    count = keys.shape[0]
    heads_q = query.astype(jnp.float32).reshape(length, HEADS, HEAD_DIM)
    heads_k = keys.astype(jnp.float32).reshape(count, HEADS, HEAD_DIM)
    scores = jnp.einsum("qhd,khd->hqk", heads_q, heads_k) * (HEAD_DIM ** -0.5)
    peak = jnp.max(scores, axis=-1, keepdims=True)
    weights = jnp.exp(scores - peak)
    return weights / jnp.sum(weights, axis=-1, keepdims=True)


def attend_forward(query, keys, values):
    length = query.shape[0]
    probs = softmax_probs(query, keys)
    probs_low = lax.optimization_barrier(probs.astype(jnp.bfloat16)).astype(jnp.float32)
    heads_v = values.astype(jnp.float32).reshape(values.shape[0], HEADS, HEAD_DIM)
    output = jnp.einsum("hqk,khd->qhd", probs_low, heads_v)
    return output.reshape(length, D).astype(jnp.bfloat16)


def attend_backward(query, keys, values, grad):
    length = query.shape[0]
    count = keys.shape[0]
    probs = softmax_probs(query, keys)
    probs_low = lax.optimization_barrier(probs.astype(jnp.bfloat16)).astype(jnp.float32)
    heads_g = grad.astype(jnp.float32).reshape(length, HEADS, HEAD_DIM)
    heads_v = values.astype(jnp.float32).reshape(count, HEADS, HEAD_DIM)
    heads_k = keys.astype(jnp.float32).reshape(count, HEADS, HEAD_DIM)
    dvals = jnp.einsum("hqk,qhd->khd", probs_low, heads_g).reshape(count, D).astype(jnp.bfloat16)
    dprob = jnp.einsum("qhd,khd->hqk", heads_g, heads_v)
    inner = jnp.sum(probs * dprob, axis=-1, keepdims=True)
    dscore = (probs * (dprob - inner) * (HEAD_DIM ** -0.5)).astype(jnp.bfloat16)
    dscore = lax.optimization_barrier(dscore).astype(jnp.float32)
    dquery = jnp.einsum("hqk,khd->qhd", dscore, heads_k).reshape(length, D).astype(jnp.bfloat16)
    return dquery, dvals


def reference(patches, query_s, key_s, value_s, query_t, key_t, value_t, adapters_a, adapters_b, cotangent):
    def flat(array):
        return array.reshape(-1, D)

    def encode(inputs, index):
        return jnp.dot(flat(inputs), adapters_a[index], preferred_element_type=jnp.float32).astype(jnp.bfloat16)

    def adapted(base, codes, index):
        lifted = flat(base).astype(jnp.float32) + jnp.dot(codes, adapters_b[index], preferred_element_type=jnp.float32)
        return lifted.astype(jnp.bfloat16)

    def to_frames(array):
        return array.reshape(CLIPS * FRAMES, PATCHES, D)

    def to_time(array):
        return array.reshape(CLIPS, FRAMES, PATCHES, D).transpose(0, 2, 1, 3).reshape(CLIPS * PATCHES, FRAMES, D)

    def from_time(array):
        return array.reshape(CLIPS, PATCHES, FRAMES, D).transpose(0, 2, 1, 3).reshape(-1, D)

    codes_sq = encode(patches, 0)
    codes_sv = encode(patches, 1)
    q_s = to_frames(adapted(query_s, codes_sq, 0))
    v_s = to_frames(adapted(value_s, codes_sv, 1))
    k_s = to_frames(key_s)
    o_s = lax.map(lambda trio: attend_forward(trio[0], trio[1], trio[2]), (q_s, k_s, v_s))
    hidden = (flat(patches).astype(jnp.float32) + flat(o_s).astype(jnp.float32)).astype(jnp.bfloat16)
    codes_tq = encode(hidden, 2)
    codes_tv = encode(hidden, 3)
    q_t = to_time(adapted(query_t, codes_tq, 2))
    v_t = to_time(adapted(value_t, codes_tv, 3))
    k_t = to_time(key_t)
    o_t = from_time(jax.vmap(attend_forward)(q_t, k_t, v_t))
    mixed = (hidden.astype(jnp.float32) + o_t.astype(jnp.float32)).astype(jnp.bfloat16)

    dq_t, dv_t = jax.vmap(attend_backward)(q_t, k_t, v_t, to_time(cotangent))
    dq_t = from_time(dq_t)
    dv_t = from_time(dv_t)

    def adapter_grads(codes, inputs, dproj, index):
        grad_b = jnp.dot(codes.T, dproj, preferred_element_type=jnp.float32)
        dcodes = jnp.dot(dproj, adapters_b[index].T, preferred_element_type=jnp.float32).astype(jnp.bfloat16)
        grad_a = jnp.dot(flat(inputs).T, dcodes, preferred_element_type=jnp.float32)
        return grad_a, grad_b, dcodes

    ga_tq, gb_tq, dcodes_tq = adapter_grads(codes_tq, hidden, dq_t, 2)
    ga_tv, gb_tv, dcodes_tv = adapter_grads(codes_tv, hidden, dv_t, 3)
    dhidden = flat(cotangent).astype(jnp.float32)
    dhidden = dhidden + jnp.dot(dcodes_tq, adapters_a[2].T, preferred_element_type=jnp.float32)
    dhidden = (dhidden + jnp.dot(dcodes_tv, adapters_a[3].T, preferred_element_type=jnp.float32)).astype(jnp.bfloat16)

    dq_s, dv_s = lax.map(lambda quad: attend_backward(quad[0], quad[1], quad[2], quad[3]), (q_s, k_s, v_s, to_frames(dhidden)))
    ga_sq, gb_sq, dcodes_sq = adapter_grads(codes_sq, patches, flat(dq_s), 0)
    ga_sv, gb_sv, dcodes_sv = adapter_grads(codes_sv, patches, flat(dv_s), 1)
    factor = (CLIPS * FRAMES * PATCHES) ** -0.5
    grads_a = jnp.stack([ga_sq, ga_sv, ga_tq, ga_tv]) * factor
    grads_b = jnp.stack([gb_sq, gb_sv, gb_tq, gb_tv]) * factor
    return mixed.reshape(CLIPS, FRAMES, PATCHES, D), grads_a, grads_b
```

```python
import math

import jax
import jax.numpy as jnp
from jax import lax
from jax.experimental import pallas as pl
from jax.experimental.pallas import tpu as pltpu
from jax.sharding import PartitionSpec as P

MESH = pl.DeviceIdType.MESH
F32 = jnp.float32
BF16 = jnp.bfloat16

HEAD_DIM = 72
HEADS = 16
D = HEADS * HEAD_DIM
TOK = 128
LENGTH = 1024
CHUNK = 256
SOURCES = 4
ZCHUNKS = 8
ZHEADS = HEADS // ZCHUNKS
SCALE = HEAD_DIM ** -0.5
FACTOR = 65536 ** -0.5
LOG2E = math.log2(math.e)

NN = (((1,), (0,)), ((), ()))
NT = (((1,), (1,)), ((), ()))
TN = (((0,), (0,)), ((), ()))


def dot(a, b, dims=NN):
    return lax.dot_general(a, b, dims, preferred_element_type=F32)


def rounded(x):
    return x.astype(BF16).astype(F32)


def half_turn(x):
    return pltpu.roll(x, 64, 1)


def low_lanes():
    return lax.broadcasted_iota(jnp.int32, (1, TOK), 1) < 64


def to_frames(a, b):
    low = low_lanes()
    return jnp.where(low, a, half_turn(b)), jnp.where(low, half_turn(a), b)


def from_frames(first, second):
    low = low_lanes()
    return jnp.where(low, first, half_turn(second)), jnp.where(low, half_turn(first), second)


def head_rows(h):
    return pl.ds(pl.multiple_of(h * HEAD_DIM, 8), HEAD_DIM)


def kernel(
    patches, query_s, key_s, value_s, query_t, key_t, value_t, cot, at, bm, ah, bh,
    mixed, ga, gb,
    t0, t1, xt, qtt, cott, ht, lv, dq5,
    send_in, recv_in, codes_all, codes_own,
    kt, kn, vt, vn, qt, cf, cc, probs, ot,
    o_send, o_recv,
    kv, ctv, dcv, dcv_own,
    dct_own, dct_all, dctf, gf, dq, dv, dcs_send, dcs_recv,
    gt_send, gt_recv, za_t, zb_t, ag_t,
    gs_send, gs_recv, za_s, zb_s, ag_s,
    s_in, r_in, s_code, r_code, s_o, r_o,
    s_z, r_z, s_sib, r_sib, s_fwd, r_fwd,
    s_ctv, r_ctv, s_dcv, r_dcv, s_dct, r_dct, s_dcs, r_dcs,
    s_gt, r_gt, s_zat, r_zat, s_zbt, r_zbt, s_agt, r_agt,
    s_gs, r_gs, s_zas, r_zas, s_zbs, r_zbs, s_ags, r_ags,
):
    dp, tm, sp = lax.axis_index("dp"), lax.axis_index("tm"), lax.axis_index("space")
    z_hi, core = tm // 2, tm % 2
    d_hi, d_lo = dp // 4, dp % 4
    pos_a, pos_b = d_lo * 2 + core, z_hi * 2 + d_hi

    def space_peer(step):
        peer = (sp + step) % 16
        return peer, (dp, tm, peer)

    def tm_peer(step):
        peer = (tm + step) % 4
        return peer, (dp, peer, sp)

    def a_peer(step):
        peer = (pos_a + step) % 8
        return peer, (d_hi * 4 + peer // 2, z_hi * 2 + peer % 2, sp)

    def b_peer(step):
        peer = (pos_b + step) % 4
        return peer, ((peer % 2) * 4 + d_lo, (peer // 2) * 2 + core, sp)

    across = (tm + 2) % 4
    sibling = z_hi * 2 + 1 - core
    far = (1 - z_hi) * 2 + 1 - core

    def copy(src, dst, s_sem, r_sem, device):
        return pltpu.make_async_remote_copy(
            src_ref=src, dst_ref=dst, send_sem=s_sem, recv_sem=r_sem, device_id=device, device_id_type=MESH
        )

    def start_all(peer_of, count, src_of, dst, s_sems, r_sems, me):
        @pl.loop(1, count)
        def _(step):
            peer, device = peer_of(step)
            copy(src_of(peer), dst.at[me], s_sems.at[peer], r_sems.at[me], device).start()

    def finish_all(peer_of, count, src_of, dst, s_sems, r_sems):
        @pl.loop(1, count)
        def _(step):
            peer, device = peer_of(step)
            done = copy(src_of(peer), dst.at[peer], s_sems.at[peer], r_sems.at[peer], device)
            done.wait_recv()
            done.wait_send()

    barrier = pltpu.get_barrier_semaphore()

    @pl.loop(1, 16)
    def _(step):
        pl.semaphore_signal(barrier, inc=1, device_id=space_peer(step)[1], device_id_type=MESH)

    @pl.loop(1, 8)
    def _(step):
        pl.semaphore_signal(barrier, inc=1, device_id=a_peer(step)[1], device_id_type=MESH)

    @pl.loop(1, 4)
    def _(step):
        pl.semaphore_signal(barrier, inc=1, device_id=b_peer(step)[1], device_id_type=MESH)

    pl.semaphore_signal(barrier, inc=1, device_id=(dp, far, sp), device_id_type=MESH)

    def transpose_in(src, dst):
        for i in range(D // 128):
            dst[pl.ds(i * 128, 128), :] = src[:, pl.ds(i * 128, 128)].astype(F32).T

    transpose_in(key_t, t0)
    transpose_in(value_t, t1)

    @pl.loop(0, HEADS)
    def _(h):
        rows = head_rows(h)
        kv[tm, h] = jnp.concatenate([t0[rows, :], t1[rows, :]], axis=0).astype(BF16)

    codes_own[...] = dot(at[pl.ds(0, 32), :], patches[...], NT).astype(BF16)
    transpose_in(key_s, t0)
    transpose_in(query_s, t1)

    @pl.loop(0, HEADS)
    def _(h):
        rows = head_rows(h)
        send_in[0, h] = jnp.concatenate([t0[rows, :], t1[rows, :]], axis=0).astype(BF16)

    pl.semaphore_wait(barrier, 15 + 7 + 3 + 1)

    def z_slot(source, c):
        return kv.at[source, pl.ds(c * ZHEADS, ZHEADS)]

    for c in range(ZCHUNKS):
        copy(z_slot(tm, c), z_slot(tm, c), s_z.at[c], r_z.at[c], (dp, across, sp)).start()
    start_all(space_peer, 16, lambda p: codes_own, codes_all, s_code, r_code, sp)
    start_all(space_peer, 16, lambda p: send_in.at[0, p], recv_in.at[0], s_in.at[0], r_in.at[0], sp)
    for c in range(ZCHUNKS):
        copy(z_slot(tm, c), z_slot(tm, c), s_sib.at[c], r_sib.at[c], (dp, sibling, sp)).start()
    transpose_in(value_s, t0)
    transpose_in(cot, cott)

    @pl.loop(0, HEADS)
    def _(h):
        rows = head_rows(h)
        send_in[1, h] = jnp.concatenate([t0[rows, :], cott[rows, :]], axis=0).astype(BF16)

    start_all(space_peer, 16, lambda p: send_in.at[1, p], recv_in.at[1], s_in.at[1], r_in.at[1], sp)
    recv_in[0, sp] = send_in[0, sp]
    recv_in[1, sp] = send_in[1, sp]
    codes_all[sp] = codes_own[...]
    transpose_in(patches, xt)
    transpose_in(query_t, qtt)

    finish_all(space_peer, 16, lambda p: codes_own, codes_all, s_code, r_code)
    for part in range(2):
        finish_all(
            space_peer, 16, lambda p: send_in.at[part, p], recv_in.at[part], s_in.at[part], r_in.at[part]
        )

    @pl.loop(0, 8)
    def _(j):
        lanes = pl.ds(pl.multiple_of(j * 128, 128), 128)
        even, odd = 2 * j, 2 * j + 1
        kq = to_frames(recv_in[0, even].astype(F32), recv_in[0, odd].astype(F32))
        vc = to_frames(recv_in[1, even].astype(F32), recv_in[1, odd].astype(F32))
        codes = to_frames(codes_all[even].astype(F32), codes_all[odd].astype(F32))
        for f in range(2):
            code = codes[f].astype(BF16)
            cc[f, :, lanes] = code
            keys = kq[f][:HEAD_DIM]
            query = kq[f][HEAD_DIM:] + dot(bh[pl.ds(0, 16), :], code[:16], TN)
            values = rounded(vc[f][:HEAD_DIM] + dot(bh[pl.ds(16, 16), :], code[16:], TN))
            kt[f, :, lanes] = keys.astype(BF16)
            kn[f, lanes, :] = keys.T.astype(BF16)
            qt[f, :, lanes] = query.astype(BF16)
            vt[f, :, lanes] = values.astype(BF16)
            vn[f, lanes, :] = values.T.astype(BF16)
            cf[f, :, lanes] = vc[f][HEAD_DIM:]

    @pl.loop(0, 2 * LENGTH // CHUNK)
    def _(i):
        f = i // (LENGTH // CHUNK)
        lanes = pl.ds(pl.multiple_of((i % (LENGTH // CHUNK)) * CHUNK, CHUNK), CHUNK)
        scores = dot(kn[f], qt[f, :, lanes])
        weights = jnp.exp2((scores - jnp.max(scores, axis=0, keepdims=True)) * (SCALE * LOG2E))
        p = weights * (1.0 / jnp.sum(weights, axis=0, keepdims=True))
        probs[f, :, lanes] = p
        ot[f, :, lanes] = dot(vt[f], p.astype(BF16))

    @pl.loop(0, 8)
    def _(j):
        lanes = pl.ds(pl.multiple_of(j * 128, 128), 128)
        pair = from_frames(ot[0, :, lanes], ot[1, :, lanes])
        for k in range(2):
            o_send[2 * j + k] = jnp.concatenate([pair[k], jnp.zeros((8, TOK), F32)], axis=0).astype(BF16)

    start_all(space_peer, 16, lambda p: o_send.at[p], o_recv, s_o, r_o, sp)
    o_recv[sp] = o_send[sp]
    finish_all(space_peer, 16, lambda p: o_send.at[p], o_recv, s_o, r_o)

    @pl.loop(0, HEADS)
    def _(h):
        rows = head_rows(h)
        ht[rows, :] = rounded(xt[rows, :] + o_recv[h].astype(F32)[:HEAD_DIM])

    hidden = ht[...].astype(BF16)
    codes_t = dot(at[pl.ds(32, 32), :], hidden).astype(BF16)
    codes_tq = codes_t[:16]
    ctv[tm] = codes_t[16:]
    start_all(tm_peer, 4, lambda p: ctv.at[tm], ctv, s_ctv, r_ctv, tm)
    qtt[...] = rounded(qtt[...] + dot(bm[pl.ds(32, 16), :], codes_tq, TN))
    finish_all(tm_peer, 4, lambda p: ctv.at[tm], ctv, s_ctv, r_ctv)
    for s in range(SOURCES):
        lv[s] = dot(bm[pl.ds(48, 16), :], ctv[s], TN)

    def temporal_head(h):
        rows = head_rows(h)
        q, g = qtt[rows, :], cott[rows, :]
        keys, values, straight, turned, d_straight, d_turned = [], [], [], [], [], []
        for s in range(SOURCES):
            both = kv[s, h].astype(F32)
            k, v = both[:HEAD_DIM], rounded(both[HEAD_DIM:] + lv[s, rows, :])
            k_r, v_r = half_turn(k), half_turn(v)
            keys.append((k, k_r))
            values.append((v, v_r))
            straight.append(jnp.sum(q * k, axis=0, keepdims=True))
            turned.append(jnp.sum(q * k_r, axis=0, keepdims=True))
            d_straight.append(jnp.sum(g * v, axis=0, keepdims=True))
            d_turned.append(jnp.sum(g * v_r, axis=0, keepdims=True))
        scores = jnp.concatenate(straight + turned, axis=0)
        weights = jnp.exp2((scores - jnp.max(scores, axis=0, keepdims=True)) * (SCALE * LOG2E))
        p = weights * (1.0 / jnp.sum(weights, axis=0, keepdims=True))
        dprob = jnp.concatenate(d_straight + d_turned, axis=0)
        inner = jnp.sum(p * dprob, axis=0, keepdims=True)
        dscore = rounded(p * (dprob - inner) * SCALE)
        low = rounded(p)
        low_r, g_r = half_turn(low), half_turn(g)
        out = jnp.zeros((HEAD_DIM, TOK), F32)
        dquery = jnp.zeros((HEAD_DIM, TOK), F32)
        for s in range(SOURCES):
            out = out + low[s : s + 1] * values[s][0] + low[s + 4 : s + 5] * values[s][1]
            dquery = dquery + dscore[s : s + 1] * keys[s][0] + dscore[s + 4 : s + 5] * keys[s][1]
            dq5[1 + s, rows, :] = low[s : s + 1] * g + low_r[s + 4 : s + 5] * g_r
        dq5[0, rows, :] = dquery
        t0[rows, :] = ht[rows, :] + rounded(out)

    for c in range(ZCHUNKS):
        copy(z_slot(tm, c), z_slot(across, c), s_z.at[c], r_z.at[c], (dp, across, sp)).wait_recv()
        copy(z_slot(across, c), z_slot(across, c), s_fwd.at[c], r_fwd.at[c], (dp, sibling, sp)).start()
        copy(z_slot(tm, c), z_slot(sibling, c), s_sib.at[c], r_sib.at[c], (dp, sibling, sp)).wait_recv()
        copy(z_slot(across, c), z_slot(far, c), s_fwd.at[c], r_fwd.at[c], (dp, sibling, sp)).wait_recv()

        @pl.loop(c * ZHEADS, (c + 1) * ZHEADS)
        def _(h):
            temporal_head(h)

    for s in range(SOURCES):
        dcv_own[s] = dot(bm[pl.ds(48, 16), :], dq5[1 + s].astype(BF16))
    start_all(tm_peer, 4, lambda p: dcv_own.at[p], dcv, s_dcv, r_dcv, tm)
    dcv[tm] = dcv_own[tm]
    dq_t = dq5[0].astype(BF16)
    dcodes_tq = dot(bm[pl.ds(32, 16), :], dq_t)
    grad_b = [dot(codes_tq, dq_t, NT)]
    part_v = dot(ctv[0], dq5[1].astype(BF16), NT)
    for s in range(1, SOURCES):
        part_v = part_v + dot(ctv[s], dq5[1 + s].astype(BF16), NT)
    grad_b.append(part_v)
    finish_all(tm_peer, 4, lambda p: dcv_own.at[p], dcv, s_dcv, r_dcv)
    dcodes_tv = dcv[0] + dcv[1] + dcv[2] + dcv[3]
    dcodes_t = jnp.concatenate([dcodes_tq, dcodes_tv], axis=0).astype(BF16)
    dct_own[...] = dcodes_t
    start_all(space_peer, 16, lambda p: dct_own, dct_all, s_dct, r_dct, sp)
    dct_all[sp] = dcodes_t

    grad_a = dot(dcodes_t, ht[...].astype(BF16), NT)
    quarters = [grad_a[:16], grad_a[16:], grad_b[0], grad_b[1]]
    for r in range(4):
        for c in range(3):
            gt_send[3 * r + c] = quarters[r][:, 384 * c : 384 * (c + 1)].astype(BF16)
    for piece in range(12, 16):
        gt_send[piece] = jnp.zeros((16, 384), BF16)
    start_all(space_peer, 16, lambda p: gt_send.at[p], gt_recv, s_gt, r_gt, sp)
    gt_recv[sp] = gt_send[sp]

    for i in range(D // 128):
        cols = pl.ds(i * 128, 128)
        mixed[:, cols] = t0[cols, :].T.astype(BF16)

    finish_all(space_peer, 16, lambda p: dct_own, dct_all, s_dct, r_dct)

    @pl.loop(0, 8)
    def _(j):
        lanes = pl.ds(pl.multiple_of(j * 128, 128), 128)
        codes = to_frames(dct_all[2 * j].astype(F32), dct_all[2 * j + 1].astype(F32))
        for f in range(2):
            gf[f, :, lanes] = (
                cf[f, :, lanes] + dot(ah[pl.ds(32, 32), :], codes[f].astype(BF16), TN)
            ).astype(BF16)

    dv[...] = jnp.zeros_like(dv)

    @pl.loop(0, 2 * LENGTH // CHUNK)
    def _(i):
        f = i // (LENGTH // CHUNK)
        lanes = pl.ds(pl.multiple_of((i % (LENGTH // CHUNK)) * CHUNK, CHUNK), CHUNK)
        g = gf[f, :, lanes]
        dprob = dot(vn[f], g)
        p = probs[f, :, lanes]
        inner = jnp.sum(p * dprob, axis=0, keepdims=True)
        dscore = (p * (dprob - inner) * SCALE).astype(BF16)
        dq[f, :, lanes] = dot(kt[f], dscore)
        dv[f] += dot(g, p.astype(BF16), NT)

    def sum_slots(ref, count):
        total = ref[0].astype(F32)
        for k in range(1, count):
            total = total + ref[k].astype(F32)
        return total

    finish_all(space_peer, 16, lambda p: gt_send.at[p], gt_recv, s_gt, r_gt)
    za_t[pos_a] = sum_slots(gt_recv, 16).astype(BF16)
    start_all(a_peer, 8, lambda p: za_t.at[pos_a], za_t, s_zat, r_zat, pos_a)

    pad = jnp.zeros((128 - HEAD_DIM, LENGTH), F32)
    gb_q = jnp.zeros((16, 128), F32)
    gb_v = jnp.zeros((16, 128), F32)
    for f in range(2):
        dq_f = jnp.concatenate([dq[f], pad], axis=0).astype(BF16)
        dv_f = jnp.concatenate([dv[f], pad], axis=0).astype(BF16)
        gb_q = gb_q + dot(cc[f, pl.ds(0, 16), :], dq_f, NT)
        gb_v = gb_v + dot(cc[f, pl.ds(16, 16), :], dv_f, NT)
        dctf[f, pl.ds(0, 16), :] = dot(bh[pl.ds(0, 16), :], dq[f].astype(BF16))
        dctf[f, pl.ds(16, 16), :] = dot(bh[pl.ds(16, 16), :], dv[f].astype(BF16))

    @pl.loop(0, 8)
    def _(j):
        lanes = pl.ds(pl.multiple_of(j * 128, 128), 128)
        pair = from_frames(dctf[0, :, lanes], dctf[1, :, lanes])
        dcs_send[2 * j] = pair[0].astype(BF16)
        dcs_send[2 * j + 1] = pair[1].astype(BF16)

    start_all(space_peer, 16, lambda p: dcs_send.at[p], dcs_recv, s_dcs, r_dcs, sp)
    dcs_recv[sp] = dcs_send[sp]

    finish_all(a_peer, 8, lambda p: za_t.at[pos_a], za_t, s_zat, r_zat)
    zb_t[pos_b] = sum_slots(za_t, 8).astype(BF16)
    start_all(b_peer, 4, lambda p: zb_t.at[pos_b], zb_t, s_zbt, r_zbt, pos_b)

    finish_all(space_peer, 16, lambda p: dcs_send.at[p], dcs_recv, s_dcs, r_dcs)
    dcodes_s = sum_slots(dcs_recv, 16).astype(BF16)
    grad_s = dot(dcodes_s, patches[...])
    for r in range(2):
        for c in range(3):
            gs_send[3 * r + c] = grad_s[16 * r : 16 * (r + 1), 384 * c : 384 * (c + 1)].astype(BF16)

    @pl.when(sp < 6)
    def _():
        gs_recv[sp] = gs_send[sp]

    @pl.loop(1, 16)
    def _(step):
        peer, device = space_peer(step)

        @pl.when(peer < 6)
        def _():
            copy(gs_send.at[peer], gs_recv.at[sp], s_gs.at[peer], r_gs.at[sp], device).start()

    finish_all(b_peer, 4, lambda p: zb_t.at[pos_b], zb_t, s_zbt, r_zbt)
    ag_t[sp] = sum_slots(zb_t, 4).astype(BF16)
    start_all(space_peer, 16, lambda p: ag_t.at[sp], ag_t, s_agt, r_agt, sp)

    za_s[pos_a, :, pl.ds(384, 128)] = gb_q.astype(BF16)
    za_s[pos_a, :, pl.ds(512, 128)] = gb_v.astype(BF16)

    @pl.when(sp < 6)
    def _():
        @pl.loop(1, 16)
        def _(step):
            peer, device = space_peer(step)
            copy(gs_send.at[0], gs_recv.at[peer], s_gs.at[0], r_gs.at[peer], device).wait_recv()

        za_s[pos_a, :, pl.ds(0, 384)] = sum_slots(gs_recv, 16).astype(BF16)

    @pl.when(sp >= 6)
    def _():
        za_s[pos_a, :, pl.ds(0, 384)] = jnp.zeros((16, 384), BF16)

    start_all(a_peer, 8, lambda p: za_s.at[pos_a], za_s, s_zas, r_zas, pos_a)

    @pl.loop(1, 16)
    def _(step):
        peer, device = space_peer(step)

        @pl.when(peer < 6)
        def _():
            copy(gs_send.at[peer], gs_recv.at[sp], s_gs.at[peer], r_gs.at[sp], device).wait_send()

    finish_all(a_peer, 8, lambda p: za_s.at[pos_a], za_s, s_zas, r_zas)
    zb_s[pos_b] = sum_slots(za_s, 8).astype(BF16)
    start_all(b_peer, 4, lambda p: zb_s.at[pos_b], zb_s, s_zbs, r_zbs, pos_b)
    finish_all(space_peer, 16, lambda p: ag_t.at[sp], ag_t, s_agt, r_agt)
    for r in range(4):
        for c in range(3):
            out = ga if r < 2 else gb
            piece = ag_t[3 * r + c].astype(F32) * FACTOR
            out[pl.ds(32 + 16 * (r % 2), 16), pl.ds(384 * c, 384)] = piece
    for c in range(ZCHUNKS):
        copy(z_slot(tm, c), z_slot(tm, c), s_z.at[c], r_z.at[c], (dp, across, sp)).wait_send()
        copy(z_slot(tm, c), z_slot(tm, c), s_sib.at[c], r_sib.at[c], (dp, sibling, sp)).wait_send()
        copy(z_slot(across, c), z_slot(across, c), s_fwd.at[c], r_fwd.at[c], (dp, sibling, sp)).wait_send()
    finish_all(b_peer, 4, lambda p: zb_s.at[pos_b], zb_s, s_zbs, r_zbs)
    ag_s[sp] = sum_slots(zb_s, 4).astype(BF16)
    start_all(space_peer, 16, lambda p: ag_s.at[sp], ag_s, s_ags, r_ags, sp)
    finish_all(space_peer, 16, lambda p: ag_s.at[sp], ag_s, s_ags, r_ags)
    for r in range(2):
        for c in range(3):
            piece = ag_s[3 * r + c, :, pl.ds(0, 384)].astype(F32) * FACTOR
            ga[pl.ds(16 * r, 16), pl.ds(384 * c, 384)] = piece
    for r in range(2):
        tiles = [jnp.zeros((16, 128), F32) for _ in range(D // 128)]
        for h in range(HEADS):
            first, offset = divmod(h * HEAD_DIM, 128)
            piece = ag_s[h, :, pl.ds(384 + 128 * r, 128)].astype(F32) * FACTOR
            if offset:
                piece = pltpu.roll(piece, offset, 1)
            lane = lax.broadcasted_iota(jnp.int32, (1, 128), 1)
            tiles[first] = tiles[first] + jnp.where(lane >= offset, piece, 0.0)
            if offset + HEAD_DIM > 128:
                tiles[first + 1] = tiles[first + 1] + jnp.where(lane < offset, piece, 0.0)
        for i in range(D // 128):
            gb[pl.ds(16 * r, 16), pl.ds(128 * i, 128)] = tiles[i]


def scratch():
    def f32(*shape):
        return pltpu.VMEM(shape, F32)

    def bf16(*shape):
        return pltpu.VMEM(shape, BF16)

    def sems(*shape):
        return pltpu.SemaphoreType.DMA(shape)

    whole = f32(D, TOK)
    return [
        whole, whole, whole, whole, whole, whole, f32(SOURCES, D, TOK), f32(1 + SOURCES, D, TOK),
        bf16(2, HEADS, 144, TOK), bf16(2, HEADS, 144, TOK), bf16(HEADS, 32, TOK), bf16(32, TOK),
        bf16(2, HEAD_DIM, LENGTH), bf16(2, LENGTH, HEAD_DIM), bf16(2, HEAD_DIM, LENGTH), bf16(2, LENGTH, HEAD_DIM),
        bf16(2, HEAD_DIM, LENGTH), f32(2, HEAD_DIM, LENGTH), bf16(2, 32, LENGTH), f32(2, LENGTH, LENGTH),
        f32(2, HEAD_DIM, LENGTH),
        bf16(HEADS, 80, TOK), bf16(HEADS, 80, TOK),
        bf16(SOURCES, HEADS, 144, TOK), bf16(SOURCES, 16, TOK), f32(SOURCES, 16, TOK), f32(SOURCES, 16, TOK),
        bf16(32, TOK), bf16(HEADS, 32, TOK), f32(2, 32, LENGTH), bf16(2, HEAD_DIM, LENGTH),
        f32(2, HEAD_DIM, LENGTH), f32(2, HEAD_DIM, LENGTH), bf16(HEADS, 32, TOK), bf16(HEADS, 32, TOK),
        bf16(16, 16, 384), bf16(16, 16, 384), bf16(8, 16, 384), bf16(4, 16, 384), bf16(16, 16, 384),
        bf16(6, 16, 384), bf16(16, 16, 384), bf16(8, 16, 640), bf16(4, 16, 640), bf16(16, 16, 640),
        sems(2, 16), sems(2, 16), sems(16), sems(16), sems(16), sems(16),
        sems(ZCHUNKS), sems(ZCHUNKS), sems(ZCHUNKS), sems(ZCHUNKS), sems(ZCHUNKS), sems(ZCHUNKS),
        sems(4), sems(4), sems(4), sems(4), sems(16), sems(16), sems(16), sems(16),
        sems(16), sems(16), sems(8), sems(8), sems(4), sems(4), sems(16), sems(16),
        sems(16), sems(16), sems(8), sems(8), sems(4), sems(4), sems(16), sems(16),
    ]


def per_device(
    patches, query_s, key_s, value_s, query_t, key_t, value_t, adapters_a, adapters_b, cotangent
):
    at = jnp.swapaxes(adapters_a, 1, 2).reshape(64, D)
    bm = adapters_b.reshape(64, D)
    start = lax.axis_index("space") * HEAD_DIM
    ah = lax.dynamic_slice_in_dim(at, start, HEAD_DIM, axis=1)
    bh = lax.dynamic_slice_in_dim(bm, start, HEAD_DIM, axis=1)
    tokens = [
        array.reshape(TOK, D)
        for array in (patches, query_s, key_s, value_s, query_t, key_t, value_t, cotangent)
    ]
    mixed, ga, gb = pl.pallas_call(
        kernel,
        out_shape=(
            jax.ShapeDtypeStruct((TOK, D), BF16),
            jax.ShapeDtypeStruct((64, D), F32),
            jax.ShapeDtypeStruct((64, D), F32),
        ),
        in_specs=[pl.BlockSpec(memory_space=pltpu.VMEM)] * 12,
        out_specs=[pl.BlockSpec(memory_space=pltpu.VMEM)] * 3,
        scratch_shapes=scratch(),
        compiler_params=pltpu.CompilerParams(
            collective_id=0, has_side_effects=True, vmem_limit_bytes=56 * 1024 * 1024
        ),
    )(*tokens, at, bm, ah, bh)
    grads_a = jnp.swapaxes(ga.reshape(4, 16, D), 1, 2)
    grads_b = gb.reshape(4, 16, D)
    return mixed.reshape(patches.shape), grads_a, grads_b


def solution(mesh):
    tokens = P("dp", "tm", "space", None)
    return jax.shard_map(
        per_device,
        mesh=mesh,
        in_specs=(tokens,) * 7 + (P(), P(), tokens),
        out_specs=(tokens, P(), P()),
        check_vma=False,
    )
```

```python
import math

import jax
import jax.numpy as jnp
from jax import lax
from jax.experimental import pallas as pl
from jax.experimental.pallas import tpu as pltpu
from jax.sharding import PartitionSpec as P

MESH = pl.DeviceIdType.MESH
F32 = jnp.float32
BF16 = jnp.bfloat16

HEAD_DIM = 72
HEADS = 16
D = HEADS * HEAD_DIM
TOK = 128
LENGTH = 1024
CHUNK = 256
SOURCES = 4
ZCHUNKS = 8
ZHEADS = HEADS // ZCHUNKS
PIECES = 18
SCALE = HEAD_DIM ** -0.5
FACTOR = 65536 ** -0.5
LOG2E = math.log2(math.e)

NN = (((1,), (0,)), ((), ()))
NT = (((1,), (1,)), ((), ()))
TN = (((0,), (0,)), ((), ()))


def dot(a, b, dims=NN):
    return lax.dot_general(a, b, dims, preferred_element_type=F32)


def rounded(x):
    return x.astype(BF16).astype(F32)


def half_turn(x):
    return pltpu.roll(x, 64, 1)


def low_lanes():
    return lax.broadcasted_iota(jnp.int32, (1, TOK), 1) < 64


def to_frames(a, b):
    low = low_lanes()
    return jnp.where(low, a, half_turn(b)), jnp.where(low, half_turn(a), b)


def from_frames(first, second):
    low = low_lanes()
    return jnp.where(low, first, half_turn(second)), jnp.where(low, half_turn(first), second)


def head_rows(h):
    return pl.ds(pl.multiple_of(h * HEAD_DIM, 8), HEAD_DIM)


def kernel(
    patches_hbm, query_s_hbm, key_s_hbm, value_s_hbm, query_t_hbm, key_t_hbm, value_t_hbm, cot_hbm, at_hbm, bm_hbm,
    mixed, ga, gb,
    patches, query_s, key_s, value_s, query_t, key_t, value_t, cot, at, bm, s_load,
    ah, bh, abt, t0, t1, xt, qtt, cott, ht, lv, dq5,
    send_in, recv_in, codes_all, codes_own,
    kt, kn, vt, vn, qt, cf, cc, probs, probs_low, ot, oe,
    o_send, o_recv,
    kv, ctv, dcv, dcv_own,
    dct_own, dct_all, dctf, gf, dq, dv, dcs_send, dcs_recv,
    gt_send, gt_recv, z_t, ag_t,
    gs_send, gs_recv, gb_send, gb_recv, z_s, ag_s,
    s_in, r_in, s_code, r_code, s_o, r_o,
    s_z, r_z, s_sib, r_sib, s_fwd, r_fwd,
    s_ctv, r_ctv, s_dcv, r_dcv, s_dct, r_dct, s_dcs, r_dcs,
    s_gt, r_gt, s_zt, r_zt, s_agt, r_agt,
    s_gs, r_gs, s_gb, r_gb, s_zs, r_zs, s_ags, r_ags,
):
    dp, tm, sp = lax.axis_index("dp"), lax.axis_index("tm"), lax.axis_index("space")
    z_hi, core = tm // 2, tm % 2
    z = z_hi * 8 + dp
    block = sp * 2 + core

    def space_peer(step):
        peer = (sp + step) % 16
        return peer, (dp, tm, peer)

    def tm_peer(step):
        peer = (tm + step) % 4
        return peer, (dp, peer, sp)

    def block_peer(step):
        peer = (block + step) % 32
        return peer, (dp, z_hi * 2 + peer % 2, peer // 2)

    def z_peer(step):
        peer = (z + step) % 16
        return peer, (peer % 8, (peer // 8) * 2 + core, sp)

    across = (tm + 2) % 4
    sibling = z_hi * 2 + 1 - core
    far = (1 - z_hi) * 2 + 1 - core

    def copy(src, dst, s_sem, r_sem, device):
        return pltpu.make_async_remote_copy(
            src_ref=src, dst_ref=dst, send_sem=s_sem, recv_sem=r_sem, device_id=device, device_id_type=MESH
        )

    def start_all(peer_of, count, src_of, dst, s_sem, r_sem, me, limit=None):
        @pl.loop(1, count)
        def _(step):
            peer, device = peer_of(step)

            def start():
                copy(src_of(peer), dst.at[me], s_sem, r_sem, device).start()

            if limit is None:
                start()
            else:
                pl.when(peer < limit)(start)

    def sent_all(peer_of, count, src_of, dst, s_sem, r_sem, me, limit=None):
        def wait(slots):
            all_slots = dst.at[pl.ds(0, slots)]
            copy(all_slots, all_slots, s_sem, r_sem, peer_of(1)[1]).wait_send()

        if limit is None:
            wait(count - 1)
        else:
            pl.when(me < limit)(lambda: wait(limit - 1))
            pl.when(me >= limit)(lambda: wait(limit))

    def received_all(peer_of, count, src_of, dst, s_sem, r_sem, me, limit=None):
        def wait(slots):
            all_slots = dst.at[pl.ds(0, slots)]
            copy(all_slots, all_slots, s_sem, r_sem, peer_of(1)[1]).wait_recv()

        if limit is None:
            wait(count - 1)
        else:
            pl.when(me < limit)(lambda: wait(limit - 1))
            pl.when(me >= limit)(lambda: wait(limit))

    barrier = pltpu.get_barrier_semaphore()
    pl.semaphore_signal(barrier, inc=1, device_id=(dp, far, sp), device_id_type=MESH)

    @pl.loop(1, 16)
    def _(step):
        pl.semaphore_signal(barrier, inc=1, device_id=z_peer(step)[1], device_id_type=MESH)

    @pl.loop(1, 32)
    def _(step):
        pl.semaphore_signal(barrier, inc=1, device_id=block_peer(step)[1], device_id_type=MESH)

    loads = {}
    for i, (src, dst) in enumerate((
        (key_t_hbm, key_t), (value_t_hbm, value_t), (patches_hbm, patches), (at_hbm, at), (key_s_hbm, key_s),
        (query_s_hbm, query_s), (value_s_hbm, value_s), (cot_hbm, cot), (bm_hbm, bm), (query_t_hbm, query_t),
    )):
        loads[id(dst)] = pltpu.make_async_copy(src, dst, s_load.at[i])
        loads[id(dst)].start()

    def transpose_in(src, dst):
        loads[id(src)].wait()
        for i in range(D // 128):
            dst[pl.ds(i * 128, 128), :] = src[:, pl.ds(i * 128, 128)].astype(F32).T

    transpose_in(key_t, t0)
    transpose_in(value_t, t1)

    @pl.loop(0, HEADS)
    def _(h):
        rows = head_rows(h)
        kv[tm, h] = jnp.concatenate([t0[rows, :], t1[rows, :]], axis=0).astype(BF16)

    loads[id(patches)].wait()
    loads[id(at)].wait()
    codes_own[...] = dot(at[pl.ds(0, 32), :], patches[...], NT).astype(BF16)
    transpose_in(key_s, t0)
    transpose_in(query_s, t1)

    @pl.loop(0, HEADS)
    def _(h):
        rows = head_rows(h)
        send_in[0, h] = jnp.concatenate([t0[rows, :], t1[rows, :]], axis=0).astype(BF16)

    pl.semaphore_wait(barrier, 1 + 15 + 31)

    def z_slot(source, c):
        return kv.at[source, pl.ds(c * ZHEADS, ZHEADS)]

    for c in range(ZCHUNKS):
        copy(z_slot(tm, c), z_slot(tm, c), s_z, r_z.at[c], (dp, across, sp)).start()
    codes_x = (space_peer, 16, lambda p: codes_own, codes_all, s_code, r_code, sp)
    start_all(*codes_x)
    in_x = [
        (space_peer, 16, lambda p: send_in.at[0, p], recv_in.at[0], s_in.at[0], r_in.at[0], sp),
        (space_peer, 16, lambda p: send_in.at[1, p], recv_in.at[1], s_in.at[1], r_in.at[1], sp),
    ]
    start_all(*in_x[0])
    own_to_sibling = copy(kv.at[tm], kv.at[tm], s_sib, r_sib, (dp, sibling, sp))
    own_to_sibling.start()
    transpose_in(value_s, t0)
    transpose_in(cot, cott)

    @pl.loop(0, HEADS)
    def _(h):
        rows = head_rows(h)
        send_in[1, h] = jnp.concatenate([t0[rows, :], cott[rows, :]], axis=0).astype(BF16)

    start_all(*in_x[1])
    recv_in[0, sp] = send_in[0, sp]
    recv_in[1, sp] = send_in[1, sp]
    codes_all[sp] = codes_own[...]
    for i in range(D // 128):
        xt[pl.ds(i * 128, 128), :] = patches[:, pl.ds(i * 128, 128)].astype(F32).T
    transpose_in(query_t, qtt)
    loads[id(bm)].wait()
    for src, dst in ((at, ah), (bm, bh)):
        for i in range(D // 128):
            abt[pl.ds(i * 128, 128), :] = src[:, pl.ds(i * 128, 128)].astype(F32).T
        dst[...] = abt[head_rows(sp), :].T.astype(BF16)

    received_all(*codes_x)
    received_all(*in_x[0])
    received_all(*in_x[1])

    @pl.loop(0, 8)
    def _(j):
        lanes = pl.ds(pl.multiple_of(j * 128, 128), 128)
        even, odd = 2 * j, 2 * j + 1
        kq = to_frames(recv_in[0, even].astype(F32), recv_in[0, odd].astype(F32))
        vc = to_frames(recv_in[1, even].astype(F32), recv_in[1, odd].astype(F32))
        codes = to_frames(codes_all[even].astype(F32), codes_all[odd].astype(F32))
        for f in range(2):
            code = codes[f].astype(BF16)
            cc[f, :, lanes] = code
            keys = kq[f][:HEAD_DIM]
            query = kq[f][HEAD_DIM:] + dot(bh[pl.ds(0, 16), :], code[:16], TN)
            values = rounded(vc[f][:HEAD_DIM] + dot(bh[pl.ds(16, 16), :], code[16:], TN))
            kt[f, :, lanes] = keys.astype(BF16)
            kn[f, lanes, :] = keys.T.astype(BF16)
            qt[f, :, lanes] = query.astype(BF16)
            vt[f, :, lanes] = values.astype(BF16)
            vn[f, lanes, :] = values.T.astype(BF16)
            cf[f, :, lanes] = vc[f][HEAD_DIM:]

    @pl.loop(0, 2 * LENGTH // CHUNK)
    def _(i):
        f = i // (LENGTH // CHUNK)
        lanes = pl.ds(pl.multiple_of((i % (LENGTH // CHUNK)) * CHUNK, CHUNK), CHUNK)
        scores = dot(kn[f], qt[f, :, lanes])
        weights = jnp.exp2((scores - jnp.max(scores, axis=0, keepdims=True)) * (SCALE * LOG2E))
        p = weights * (1.0 / jnp.sum(weights, axis=0, keepdims=True))
        low = p.astype(BF16)
        probs[f, :, lanes] = p * SCALE
        probs_low[f, :, lanes] = low
        out = dot(vt[f], low)
        ot[f, :, lanes] = out
        oe[f, :, lanes] = out + dot(vt[f], (p - low.astype(F32)).astype(BF16))

    @pl.loop(0, 8)
    def _(j):
        lanes = pl.ds(pl.multiple_of(j * 128, 128), 128)
        pair = from_frames(ot[0, :, lanes], ot[1, :, lanes])
        for k in range(2):
            o_send[2 * j + k] = jnp.concatenate([pair[k], jnp.zeros((8, TOK), F32)], axis=0).astype(BF16)

    o_x = (space_peer, 16, lambda p: o_send.at[p], o_recv, s_o, r_o, sp)
    start_all(*o_x)
    o_recv[sp] = o_send[sp]
    sent_all(*codes_x)
    sent_all(*in_x[0])
    sent_all(*in_x[1])
    received_all(*o_x)

    @pl.loop(0, HEADS)
    def _(h):
        rows = head_rows(h)
        ht[rows, :] = rounded(xt[rows, :] + o_recv[h].astype(F32)[:HEAD_DIM])

    hidden = ht[...].astype(BF16)
    codes_t = dot(at[pl.ds(32, 32), :], hidden).astype(BF16)
    codes_tq = codes_t[:16]
    ctv[tm] = codes_t[16:]
    ctv_x = (tm_peer, 4, lambda p: ctv.at[tm], ctv, s_ctv, r_ctv, tm)
    start_all(*ctv_x)
    sent_all(*o_x)
    qtt[...] = rounded(qtt[...] + dot(bm[pl.ds(32, 16), :], codes_tq, TN))
    received_all(*ctv_x)
    for s in range(SOURCES):
        lv[s] = dot(bm[pl.ds(48, 16), :], ctv[s], TN)

    def temporal_head(h):
        rows = head_rows(h)
        q, g = qtt[rows, :], cott[rows, :]
        keys, values, straight, turned, d_straight, d_turned = [], [], [], [], [], []
        for s in range(SOURCES):
            both = kv[s, h].astype(F32)
            k, v = both[:HEAD_DIM], rounded(both[HEAD_DIM:] + lv[s, rows, :])
            k_r, v_r = half_turn(k), half_turn(v)
            keys.append((k, k_r))
            values.append((v, v_r))
            straight.append(jnp.sum(q * k, axis=0, keepdims=True))
            turned.append(jnp.sum(q * k_r, axis=0, keepdims=True))
            d_straight.append(jnp.sum(g * v, axis=0, keepdims=True))
            d_turned.append(jnp.sum(g * v_r, axis=0, keepdims=True))
        scores = jnp.concatenate(straight + turned, axis=0)
        weights = jnp.exp2((scores - jnp.max(scores, axis=0, keepdims=True)) * (SCALE * LOG2E))
        p = weights * (1.0 / jnp.sum(weights, axis=0, keepdims=True))
        dprob = jnp.concatenate(d_straight + d_turned, axis=0)
        inner = jnp.sum(p * dprob, axis=0, keepdims=True)
        dscore = rounded(p * (dprob - inner) * SCALE)
        low = rounded(p)
        low_r, g_r = half_turn(low), half_turn(g)
        out = jnp.zeros((HEAD_DIM, TOK), F32)
        dquery = jnp.zeros((HEAD_DIM, TOK), F32)
        for s in range(SOURCES):
            out = out + low[s : s + 1] * values[s][0] + low[s + 4 : s + 5] * values[s][1]
            dquery = dquery + dscore[s : s + 1] * keys[s][0] + dscore[s + 4 : s + 5] * keys[s][1]
            dq5[1 + s, rows, :] = low[s : s + 1] * g + low_r[s + 4 : s + 5] * g_r
        dq5[0, rows, :] = dquery
        t0[rows, :] = ht[rows, :] + rounded(out)

    own_to_sibling.wait_recv()
    for c in range(ZCHUNKS):
        copy(z_slot(tm, c), z_slot(across, c), s_z, r_z.at[c], (dp, across, sp)).wait_recv()
        copy(z_slot(across, c), z_slot(across, c), s_fwd, r_fwd.at[c], (dp, sibling, sp)).start()
        copy(z_slot(across, c), z_slot(far, c), s_fwd, r_fwd.at[c], (dp, sibling, sp)).wait_recv()

        @pl.loop(c * ZHEADS, (c + 1) * ZHEADS)
        def _(h):
            temporal_head(h)

    for s in range(SOURCES):
        dcv_own[s] = dot(bm[pl.ds(48, 16), :], dq5[1 + s].astype(BF16))
    dcv_x = (tm_peer, 4, lambda p: dcv_own.at[p], dcv, s_dcv, r_dcv, tm)
    start_all(*dcv_x)
    sent_all(*ctv_x)
    dcv[tm] = dcv_own[tm]
    dq_t = dq5[0].astype(BF16)
    dcodes_tq = dot(bm[pl.ds(32, 16), :], dq_t)
    grad_b = [dot(codes_tq, dq_t, NT)]
    part_v = dot(ctv[0], dq5[1].astype(BF16), NT)
    for s in range(1, SOURCES):
        part_v = part_v + dot(ctv[s], dq5[1 + s].astype(BF16), NT)
    grad_b.append(part_v)
    copy(kv.at[tm], kv.at[tm], s_z, r_z.at[0], (dp, across, sp)).wait_send()
    own_to_sibling.wait_send()
    copy(kv.at[across], kv.at[across], s_fwd, r_fwd.at[0], (dp, sibling, sp)).wait_send()
    received_all(*dcv_x)
    dcodes_tv = dcv[0] + dcv[1] + dcv[2] + dcv[3]
    dcodes_t = jnp.concatenate([dcodes_tq, dcodes_tv], axis=0).astype(BF16)
    dct_own[...] = dcodes_t
    dct_x = (space_peer, 16, lambda p: dct_own, dct_all, s_dct, r_dct, sp)
    start_all(*dct_x)
    dct_all[sp] = dcodes_t

    grad_a = dot(dcodes_t, ht[...].astype(BF16), NT)
    halves = [grad_a, jnp.concatenate(grad_b, axis=0)]
    for r in range(2):
        for c in range(9):
            gt_send[9 * r + c] = halves[r][:, 128 * c : 128 * (c + 1)].astype(BF16)
    gt_x = (block_peer, 32, lambda p: gt_send.at[p], gt_recv, s_gt, r_gt, block, PIECES)
    start_all(*gt_x)

    for i in range(D // 128):
        cols = pl.ds(i * 128, 128)
        mixed[:, cols] = t0[cols, :].T.astype(BF16)

    sent_all(*dcv_x)
    received_all(*dct_x)

    @pl.loop(0, 8)
    def _(j):
        lanes = pl.ds(pl.multiple_of(j * 128, 128), 128)
        codes = to_frames(dct_all[2 * j].astype(F32), dct_all[2 * j + 1].astype(F32))
        for f in range(2):
            gf[f, :, lanes] = (
                cf[f, :, lanes] + dot(ah[pl.ds(32, 32), :], codes[f].astype(BF16), TN)
            ).astype(BF16)

    dv[...] = jnp.zeros_like(dv)

    def backward(f):
        @pl.loop(0, LENGTH // CHUNK)
        def _(i):
            lanes = pl.ds(pl.multiple_of(i * CHUNK, CHUNK), CHUNK)
            g = gf[f, :, lanes]
            inner = jnp.sum(g.astype(F32) * oe[f, :, lanes], axis=0, keepdims=True)
            dprob = dot(vn[f], g)
            dscore = (probs[f, :, lanes] * (dprob - inner)).astype(BF16)
            dq[f, :, lanes] = dot(kt[f], dscore)
            dv[f] += dot(g, probs_low[f, :, lanes], NT)

    def sum_slots(ref, count):
        total = ref[0].astype(F32)
        for k in range(1, count):
            total = total + ref[k].astype(F32)
        return total

    backward(0)
    z_t_x = (z_peer, 16, lambda p: z_t.at[z], z_t, s_zt, r_zt, z)

    @pl.when(block < PIECES)
    def _():
        gt_recv[block] = gt_send[block]
        received_all(block_peer, 32, lambda p: gt_send.at[p], gt_recv, s_gt, r_gt, block)
        z_t[z] = sum_slots(gt_recv, 32).astype(BF16)
        start_all(*z_t_x)

    backward(1)
    pad = jnp.zeros((128 - HEAD_DIM, LENGTH), F32)
    gb_q = jnp.zeros((16, 128), F32)
    gb_v = jnp.zeros((16, 128), F32)
    for f in range(2):
        dctf[f, pl.ds(0, 16), :] = dot(bh[pl.ds(0, 16), :], dq[f].astype(BF16))
        dctf[f, pl.ds(16, 16), :] = dot(bh[pl.ds(16, 16), :], dv[f].astype(BF16))

    @pl.loop(0, 8)
    def _(j):
        lanes = pl.ds(pl.multiple_of(j * 128, 128), 128)
        pair = from_frames(dctf[0, :, lanes], dctf[1, :, lanes])
        dcs_send[2 * j] = pair[0].astype(BF16)
        dcs_send[2 * j + 1] = pair[1].astype(BF16)

    dcs_x = (space_peer, 16, lambda p: dcs_send.at[p], dcs_recv, s_dcs, r_dcs, sp)
    start_all(*dcs_x)
    dcs_recv[sp] = dcs_send[sp]
    for f in range(2):
        dq_f = jnp.concatenate([dq[f], pad], axis=0).astype(BF16)
        dv_f = jnp.concatenate([dv[f], pad], axis=0).astype(BF16)
        gb_q = gb_q + dot(cc[f, pl.ds(0, 16), :], dq_f, NT)
        gb_v = gb_v + dot(cc[f, pl.ds(16, 16), :], dv_f, NT)
    gb_send[0] = gb_q.astype(BF16)
    gb_send[1] = gb_v.astype(BF16)
    to_sibling = copy(gb_send.at[1 - core], gb_recv, s_gb, r_gb, (dp, sibling, sp))
    to_sibling.start()
    sent_all(*dct_x)
    sent_all(*gt_x)
    received_all(*dcs_x)
    dcodes_s = sum_slots(dcs_recv, 16).astype(BF16)
    grad_s = dot(dcodes_s, patches[...])
    for r in range(2):
        for c in range(9):
            gs_send[9 * r + c] = grad_s[16 * r : 16 * (r + 1), 128 * c : 128 * (c + 1)].astype(BF16)
    gs_x = (block_peer, 32, lambda p: gs_send.at[p], gs_recv, s_gs, r_gs, block, PIECES)
    start_all(*gs_x)
    sent_all(*dcs_x)
    to_sibling.wait_recv()
    z_s[z, pl.ds(16, 16), :] = (gb_send[core].astype(F32) + gb_recv[...].astype(F32)).astype(BF16)

    @pl.when(block < PIECES)
    def _():
        received_all(*z_t_x)
        ag_t[block] = sum_slots(z_t, 16).astype(BF16)
        gs_recv[block] = gs_send[block]
        received_all(block_peer, 32, lambda p: gs_send.at[p], gs_recv, s_gs, r_gs, block)
        z_s[z, pl.ds(0, 16), :] = sum_slots(gs_recv, 32).astype(BF16)

    @pl.when(block >= PIECES)
    def _():
        z_s[z, pl.ds(0, 16), :] = jnp.zeros((16, 128), BF16)

    z_s_x = (z_peer, 16, lambda p: z_s.at[z], z_s, s_zs, r_zs, z)
    start_all(*z_s_x)
    ag_t_x = (block_peer, 32, lambda p: ag_t.at[block], ag_t, s_agt, r_agt, block)

    @pl.when(block < PIECES)
    def _():
        start_all(*ag_t_x)
        sent_all(*z_t_x)

    sent_all(*gs_x)
    to_sibling.wait_send()
    received_all(*ag_t_x, PIECES)
    for piece in range(PIECES):
        out = (ga, gb)[piece // 9]
        out[pl.ds(32, 32), pl.ds(128 * (piece % 9), 128)] = ag_t[piece].astype(F32) * FACTOR

    @pl.when(block < PIECES)
    def _():
        sent_all(*ag_t_x)

    received_all(*z_s_x)
    ag_s[block] = sum_slots(z_s, 16).astype(BF16)
    ag_s_x = (block_peer, 32, lambda p: ag_s.at[block], ag_s, s_ags, r_ags, block)
    start_all(*ag_s_x)
    sent_all(*z_s_x)
    received_all(*ag_s_x)
    for piece in range(PIECES):
        rows = pl.ds(16 * (piece // 9), 16)
        ga[rows, pl.ds(128 * (piece % 9), 128)] = ag_s[piece, pl.ds(0, 16), :].astype(F32) * FACTOR
    for r in range(2):
        tiles = [jnp.zeros((16, 128), F32) for _ in range(D // 128)]
        for h in range(HEADS):
            first, offset = divmod(h * HEAD_DIM, 128)
            piece = ag_s[2 * h + r, pl.ds(16, 16), :].astype(F32) * FACTOR
            if offset:
                piece = pltpu.roll(piece, offset, 1)
            lane = lax.broadcasted_iota(jnp.int32, (1, 128), 1)
            tiles[first] = tiles[first] + jnp.where(lane >= offset, piece, 0.0)
            if offset + HEAD_DIM > 128:
                tiles[first + 1] = tiles[first + 1] + jnp.where(lane < offset, piece, 0.0)
        for i in range(D // 128):
            gb[pl.ds(16 * r, 16), pl.ds(128 * i, 128)] = tiles[i]
    sent_all(*ag_s_x)


def scratch():
    def f32(*shape):
        return pltpu.VMEM(shape, F32)

    def bf16(*shape):
        return pltpu.VMEM(shape, BF16)

    def sems(*shape):
        return pltpu.SemaphoreType.DMA(shape)

    whole = f32(D, TOK)
    one = pltpu.SemaphoreType.DMA
    return [
        *[bf16(TOK, D)] * 8, bf16(64, D), bf16(64, D), sems(10),
        bf16(64, HEAD_DIM), bf16(64, HEAD_DIM), f32(D, 64),
        whole, whole, whole, whole, whole, whole, f32(SOURCES, D, TOK), f32(1 + SOURCES, D, TOK),
        bf16(2, HEADS, 144, TOK), bf16(2, HEADS, 144, TOK), bf16(HEADS, 32, TOK), bf16(32, TOK),
        bf16(2, HEAD_DIM, LENGTH), bf16(2, LENGTH, HEAD_DIM), bf16(2, HEAD_DIM, LENGTH), bf16(2, LENGTH, HEAD_DIM),
        bf16(2, HEAD_DIM, LENGTH), f32(2, HEAD_DIM, LENGTH), bf16(2, 32, LENGTH), f32(2, LENGTH, LENGTH),
        bf16(2, LENGTH, LENGTH), f32(2, HEAD_DIM, LENGTH), f32(2, HEAD_DIM, LENGTH),
        bf16(HEADS, 80, TOK), bf16(HEADS, 80, TOK),
        bf16(SOURCES, HEADS, 144, TOK), bf16(SOURCES, 16, TOK), f32(SOURCES, 16, TOK), f32(SOURCES, 16, TOK),
        bf16(32, TOK), bf16(HEADS, 32, TOK), f32(2, 32, LENGTH), bf16(2, HEAD_DIM, LENGTH),
        f32(2, HEAD_DIM, LENGTH), f32(2, HEAD_DIM, LENGTH), bf16(HEADS, 32, TOK), bf16(HEADS, 32, TOK),
        bf16(PIECES, 32, 128), bf16(32, 32, 128), bf16(16, 32, 128), bf16(32, 32, 128),
        bf16(PIECES, 16, 128), bf16(32, 16, 128), bf16(2, 16, 128), bf16(16, 128), bf16(16, 32, 128), bf16(32, 32, 128),
        sems(2), sems(2), one, one, one, one,
        one, sems(ZCHUNKS), one, one, one, sems(ZCHUNKS),
        one, one, one, one, one, one, one, one,
        one, one, one, one, one, one,
        one, one, one, one, one, one, one, one,
    ]


def hand_over(mixed, ga, gb, mixed_out, ga_out, gb_out):
    mixed_out[...] = mixed[...]
    ga_out[...] = ga[...]
    gb_out[...] = gb[...]


def per_device(
    patches, query_s, key_s, value_s, query_t, key_t, value_t, adapters_a, adapters_b, cotangent
):
    at = jnp.swapaxes(adapters_a, 1, 2).reshape(64, D)
    bm = adapters_b.reshape(64, D)
    tokens = [
        array.reshape(TOK, D)
        for array in (patches, query_s, key_s, value_s, query_t, key_t, value_t, cotangent)
    ]
    out_shape = (
        jax.ShapeDtypeStruct((TOK, D), BF16),
        jax.ShapeDtypeStruct((64, D), F32),
        jax.ShapeDtypeStruct((64, D), F32),
    )
    results = pl.pallas_call(
        kernel,
        out_shape=out_shape,
        in_specs=[pl.BlockSpec(memory_space=pl.ANY)] * 10,
        out_specs=[pl.BlockSpec(memory_space=pltpu.VMEM)] * 3,
        scratch_shapes=scratch(),
        compiler_params=pltpu.CompilerParams(
            collective_id=0, has_side_effects=True, vmem_limit_bytes=56 * 1024 * 1024
        ),
    )(*tokens, at, bm)
    mixed, ga, gb = pl.pallas_call(
        hand_over,
        out_shape=out_shape,
        in_specs=[pl.BlockSpec(memory_space=pltpu.VMEM)] * 3,
        out_specs=[pl.BlockSpec(memory_space=pltpu.VMEM)] * 3,
    )(*results)
    grads_a = jnp.swapaxes(ga.reshape(4, 16, D), 1, 2)
    grads_b = gb.reshape(4, 16, D)
    return mixed.reshape(patches.shape), grads_a, grads_b


def solution(mesh):
    tokens = P("dp", "tm", "space", None)
    return jax.shard_map(
        per_device,
        mesh=mesh,
        in_specs=(tokens,) * 7 + (P(), P(), tokens),
        out_specs=(tokens, P(), P()),
        check_vma=False,
    )
```

```python
import math

import jax
import jax.numpy as jnp
from jax import lax
from jax.experimental import pallas as pl
from jax.experimental.pallas import tpu as pltpu
from jax.sharding import PartitionSpec as P

MESH = pl.DeviceIdType.MESH
F32 = jnp.float32
BF16 = jnp.bfloat16

HEAD_DIM = 72
HEADS = 16
D = HEADS * HEAD_DIM
TOK = 128
LENGTH = 1024
CHUNK = 1024
SOURCES = 4
ZCHUNKS = 8
ZHEADS = HEADS // ZCHUNKS
PIECES = 18
SCALE = HEAD_DIM ** -0.5
FACTOR = 65536 ** -0.5
LOG2E = math.log2(math.e)

NN = (((1,), (0,)), ((), ()))
NT = (((1,), (1,)), ((), ()))
TN = (((0,), (0,)), ((), ()))


def dot(a, b, dims=NN):
    return lax.dot_general(a, b, dims, preferred_element_type=F32)


def rounded(x):
    return x.astype(BF16).astype(F32)


def half_turn(x):
    return pltpu.roll(x, 64, 1)


def low_lanes():
    return lax.broadcasted_iota(jnp.int32, (1, TOK), 1) < 64


def to_frames(a, b):
    low = low_lanes()
    return jnp.where(low, a, half_turn(b)), jnp.where(low, half_turn(a), b)


def from_frames(first, second):
    low = low_lanes()
    return jnp.where(low, first, half_turn(second)), jnp.where(low, half_turn(first), second)


def head_rows(h):
    return pl.ds(pl.multiple_of(h * HEAD_DIM, 8), HEAD_DIM)


def kernel(
    patches_hbm, query_s_hbm, key_s_hbm, value_s_hbm, query_t_hbm, key_t_hbm, value_t_hbm, cot_hbm, at_hbm, bm_hbm,
    mixed, ga, gb,
    patches, query_s, key_s, value_s, query_t, key_t, value_t, cot, at, bm, s_load,
    ah, bh, abt, t0, t1, xt, qtt, cott, ht, lv, dq5,
    send_kq, recv_kq, send_v, recv_v, send_c, recv_c, codes_all, codes_own,
    kt, kn, vt, vn, qt, cf, cc, probs, probs_low, ot, oe,
    o_send, o_recv,
    kv, ctv, dcv, dcv_own,
    dct_own, dct_all, dctf, gf, dq, dv, dcs_send, dcs_recv,
    gt_send, gt_recv, z_t, ag_t,
    gs_send, gs_recv, gb_send, gb_recv, z_s, ag_s,
    s_in, r_in, s_code, r_code, s_o, r_o,
    s_z, r_z, s_sib, r_sib, s_fwd, r_fwd,
    s_ctv, r_ctv, s_dcv, r_dcv, s_dct, r_dct, s_dcs, r_dcs,
    s_gt, r_gt, s_zt, r_zt, s_agt, r_agt,
    s_gs, r_gs, s_gb, r_gb, s_zs, r_zs, s_ags, r_ags,
):
    dp, tm, sp = lax.axis_index("dp"), lax.axis_index("tm"), lax.axis_index("space")
    z_hi, core = tm // 2, tm % 2
    z = z_hi * 8 + dp
    block = sp * 2 + core

    def space_peer(step):
        peer = (sp + step) % 16
        return peer, (dp, tm, peer)

    def tm_peer(step):
        peer = (tm + step) % 4
        return peer, (dp, peer, sp)

    def block_peer(step):
        peer = (block + step) % 32
        return peer, (dp, z_hi * 2 + peer % 2, peer // 2)

    def z_peer(step):
        peer = (z + step) % 16
        return peer, (peer % 8, (peer // 8) * 2 + core, sp)

    across = (tm + 2) % 4
    sibling = z_hi * 2 + 1 - core
    far = (1 - z_hi) * 2 + 1 - core

    def copy(src, dst, s_sem, r_sem, device):
        return pltpu.make_async_remote_copy(
            src_ref=src, dst_ref=dst, send_sem=s_sem, recv_sem=r_sem, device_id=device, device_id_type=MESH
        )

    def start_all(peer_of, count, src_of, dst, s_sem, r_sem, me, limit=None):
        @pl.loop(1, count)
        def _(step):
            peer, device = peer_of(step)

            def start():
                copy(src_of(peer), dst.at[me], s_sem, r_sem, device).start()

            if limit is None:
                start()
            else:
                pl.when(peer < limit)(start)

    def sent_all(peer_of, count, src_of, dst, s_sem, r_sem, me, limit=None):
        def wait(slots):
            all_slots = dst.at[pl.ds(0, slots)]
            copy(all_slots, all_slots, s_sem, r_sem, peer_of(1)[1]).wait_send()

        if limit is None:
            wait(count - 1)
        else:
            pl.when(me < limit)(lambda: wait(limit - 1))
            pl.when(me >= limit)(lambda: wait(limit))

    def received_all(peer_of, count, src_of, dst, s_sem, r_sem, me, limit=None):
        def wait(slots):
            all_slots = dst.at[pl.ds(0, slots)]
            copy(all_slots, all_slots, s_sem, r_sem, peer_of(1)[1]).wait_recv()

        if limit is None:
            wait(count - 1)
        else:
            pl.when(me < limit)(lambda: wait(limit - 1))
            pl.when(me >= limit)(lambda: wait(limit))

    barrier = pltpu.get_barrier_semaphore()
    pl.semaphore_signal(barrier, inc=1, device_id=(dp, far, sp), device_id_type=MESH)

    @pl.loop(1, 16)
    def _(step):
        pl.semaphore_signal(barrier, inc=1, device_id=z_peer(step)[1], device_id_type=MESH)

    @pl.loop(1, 32)
    def _(step):
        pl.semaphore_signal(barrier, inc=1, device_id=block_peer(step)[1], device_id_type=MESH)

    loads = {}
    for i, (src, dst) in enumerate((
        (key_t_hbm, key_t), (value_t_hbm, value_t), (patches_hbm, patches), (at_hbm, at), (key_s_hbm, key_s),
        (query_s_hbm, query_s), (value_s_hbm, value_s), (cot_hbm, cot), (bm_hbm, bm), (query_t_hbm, query_t),
    )):
        loads[id(dst)] = pltpu.make_async_copy(src, dst, s_load.at[i])
        loads[id(dst)].start()

    def transpose_in(src, dst):
        loads[id(src)].wait()
        for i in range(D // 128):
            dst[pl.ds(i * 128, 128), :] = src[:, pl.ds(i * 128, 128)].astype(F32).T

    transpose_in(key_t, t0)
    transpose_in(value_t, t1)

    @pl.loop(0, HEADS)
    def _(h):
        rows = head_rows(h)
        kv[tm, h] = jnp.concatenate([t0[rows, :], t1[rows, :]], axis=0).astype(BF16)

    loads[id(patches)].wait()
    loads[id(at)].wait()
    codes_own[...] = dot(at[pl.ds(0, 32), :], patches[...], NT).astype(BF16)
    transpose_in(key_s, t0)
    transpose_in(query_s, t1)

    @pl.loop(0, HEADS)
    def _(h):
        rows = head_rows(h)
        send_kq[h] = jnp.concatenate([t0[rows, :], t1[rows, :]], axis=0).astype(BF16)

    pl.semaphore_wait(barrier, 1 + 15 + 31)

    def z_slot(source, c):
        return kv.at[source, pl.ds(c * ZHEADS, ZHEADS)]

    def send_chunk(c):
        copy(z_slot(tm, c), z_slot(tm, c), s_z, r_z.at[c], (dp, across, sp)).start()

    for c in range(ZCHUNKS):
        send_chunk(c)
    codes_x = (space_peer, 16, lambda p: codes_own, codes_all, s_code, r_code, sp)
    start_all(*codes_x)
    kq_x = (space_peer, 16, lambda p: send_kq.at[p], recv_kq, s_in.at[0], r_in.at[0], sp)
    v_x = (space_peer, 16, lambda p: send_v.at[p], recv_v, s_in.at[1], r_in.at[1], sp)
    c_x = (space_peer, 16, lambda p: send_c.at[p], recv_c, s_in.at[2], r_in.at[2], sp)
    start_all(*kq_x)
    own_to_sibling = copy(kv.at[tm], kv.at[tm], s_sib, r_sib, (dp, sibling, sp))
    own_to_sibling.start()
    gap = jnp.zeros((8, TOK), F32)

    def pack(src, dst):
        @pl.loop(0, HEADS)
        def _(h):
            dst[h] = jnp.concatenate([src[head_rows(h), :], gap], axis=0).astype(BF16)

    transpose_in(value_s, t0)
    pack(t0, send_v)
    start_all(*v_x)
    transpose_in(cot, cott)
    pack(cott, send_c)
    recv_kq[sp] = send_kq[sp]
    recv_v[sp] = send_v[sp]
    recv_c[sp] = send_c[sp]
    codes_all[sp] = codes_own[...]
    for i in range(D // 128):
        xt[pl.ds(i * 128, 128), :] = patches[:, pl.ds(i * 128, 128)].astype(F32).T
    transpose_in(query_t, qtt)
    loads[id(bm)].wait()
    for src, dst in ((at, ah), (bm, bh)):
        for i in range(D // 128):
            abt[pl.ds(i * 128, 128), :] = src[:, pl.ds(i * 128, 128)].astype(F32).T
        dst[...] = abt[head_rows(sp), :].T.astype(BF16)

    received_all(*codes_x)
    received_all(*kq_x)
    received_all(*v_x)

    @pl.loop(0, 8)
    def _(j):
        lanes = pl.ds(pl.multiple_of(j * 128, 128), 128)
        even, odd = 2 * j, 2 * j + 1
        kq = to_frames(recv_kq[even].astype(F32), recv_kq[odd].astype(F32))
        value = to_frames(recv_v[even].astype(F32), recv_v[odd].astype(F32))
        codes = to_frames(codes_all[even].astype(F32), codes_all[odd].astype(F32))
        for f in range(2):
            code = codes[f].astype(BF16)
            cc[f, :, lanes] = code
            keys = kq[f][:HEAD_DIM]
            query = kq[f][HEAD_DIM:] + dot(bh[pl.ds(0, 16), :], code[:16], TN)
            values = rounded(value[f][:HEAD_DIM] + dot(bh[pl.ds(16, 16), :], code[16:], TN))
            kt[f, :, lanes] = keys.astype(BF16)
            kn[f, lanes, :] = keys.T.astype(BF16)
            qt[f, :, lanes] = query.astype(BF16)
            vt[f, :, lanes] = values.astype(BF16)
            vn[f, lanes, :] = values.T.astype(BF16)

    def forward(f):
        @pl.loop(0, LENGTH // CHUNK)
        def _(i):
            lanes = pl.ds(pl.multiple_of(i * CHUNK, CHUNK), CHUNK)
            scores = dot(kn[f], qt[f, :, lanes])
            weights = jnp.exp2((scores - jnp.max(scores, axis=0, keepdims=True)) * (SCALE * LOG2E))
            p = weights * (1.0 / jnp.sum(weights, axis=0, keepdims=True))
            low = p.astype(BF16)
            probs[f, :, lanes] = p * SCALE
            probs_low[f, :, lanes] = low
            out = dot(vt[f], low)
            ot[f, :, lanes] = out
            oe[f, :, lanes] = out + dot(vt[f], (p - low.astype(F32)).astype(BF16))

    forward(0)
    forward(1)

    @pl.loop(0, 8)
    def _(j):
        lanes = pl.ds(pl.multiple_of(j * 128, 128), 128)
        pair = from_frames(ot[0, :, lanes], ot[1, :, lanes])
        for k in range(2):
            o_send[2 * j + k] = jnp.concatenate([pair[k], jnp.zeros((8, TOK), F32)], axis=0).astype(BF16)

    o_x = (space_peer, 16, lambda p: o_send.at[p], o_recv, s_o, r_o, sp)
    start_all(*o_x)
    o_recv[sp] = o_send[sp]
    sent_all(*codes_x)
    sent_all(*kq_x)
    sent_all(*v_x)
    received_all(*o_x)
    start_all(*c_x)

    @pl.loop(0, HEADS)
    def _(h):
        rows = head_rows(h)
        ht[rows, :] = rounded(xt[rows, :] + o_recv[h].astype(F32)[:HEAD_DIM])

    hidden = ht[...].astype(BF16)
    codes_t = dot(at[pl.ds(32, 32), :], hidden).astype(BF16)
    codes_tq = codes_t[:16]
    ctv[tm] = codes_t[16:]
    ctv_x = (tm_peer, 4, lambda p: ctv.at[tm], ctv, s_ctv, r_ctv, tm)
    start_all(*ctv_x)
    sent_all(*o_x)
    qtt[...] = rounded(qtt[...] + dot(bm[pl.ds(32, 16), :], codes_tq, TN))
    received_all(*ctv_x)
    for s in range(SOURCES):
        lv[s] = dot(bm[pl.ds(48, 16), :], ctv[s], TN)

    def temporal_head(h):
        rows = head_rows(h)
        q, g = qtt[rows, :], cott[rows, :]
        keys, values, straight, turned, d_straight, d_turned = [], [], [], [], [], []
        for s in range(SOURCES):
            both = kv[s, h].astype(F32)
            k, v = both[:HEAD_DIM], rounded(both[HEAD_DIM:] + lv[s, rows, :])
            k_r, v_r = half_turn(k), half_turn(v)
            keys.append((k, k_r))
            values.append((v, v_r))
            straight.append(jnp.sum(q * k, axis=0, keepdims=True))
            turned.append(jnp.sum(q * k_r, axis=0, keepdims=True))
            d_straight.append(jnp.sum(g * v, axis=0, keepdims=True))
            d_turned.append(jnp.sum(g * v_r, axis=0, keepdims=True))
        scores = jnp.concatenate(straight + turned, axis=0)
        weights = jnp.exp2((scores - jnp.max(scores, axis=0, keepdims=True)) * (SCALE * LOG2E))
        p = weights * (1.0 / jnp.sum(weights, axis=0, keepdims=True))
        dprob = jnp.concatenate(d_straight + d_turned, axis=0)
        inner = jnp.sum(p * dprob, axis=0, keepdims=True)
        dscore = rounded(p * (dprob - inner) * SCALE)
        low = rounded(p)
        low_r, g_r = half_turn(low), half_turn(g)
        out = jnp.zeros((HEAD_DIM, TOK), F32)
        dquery = jnp.zeros((HEAD_DIM, TOK), F32)
        for s in range(SOURCES):
            out = out + low[s : s + 1] * values[s][0] + low[s + 4 : s + 5] * values[s][1]
            dquery = dquery + dscore[s : s + 1] * keys[s][0] + dscore[s + 4 : s + 5] * keys[s][1]
            dq5[1 + s, rows, :] = low[s : s + 1] * g + low_r[s + 4 : s + 5] * g_r
        dq5[0, rows, :] = dquery
        t0[rows, :] = ht[rows, :] + rounded(out)

    own_to_sibling.wait_recv()

    def relay_chunk(c):
        copy(z_slot(tm, c), z_slot(across, c), s_z, r_z.at[c], (dp, across, sp)).wait_recv()
        copy(z_slot(across, c), z_slot(across, c), s_fwd, r_fwd.at[c], (dp, sibling, sp)).start()

    sent_all(*c_x)
    received_all(*c_x)

    @pl.loop(0, 8)
    def _(j):
        lanes = pl.ds(pl.multiple_of(j * 128, 128), 128)
        even, odd = 2 * j, 2 * j + 1
        grad = to_frames(recv_c[even].astype(F32), recv_c[odd].astype(F32))
        for f in range(2):
            cf[f, :, lanes] = grad[f][:HEAD_DIM]

    relay_chunk(0)
    for c in range(ZCHUNKS):
        if c + 1 < ZCHUNKS:
            relay_chunk(c + 1)
        copy(z_slot(across, c), z_slot(far, c), s_fwd, r_fwd.at[c], (dp, sibling, sp)).wait_recv()

        @pl.loop(c * ZHEADS, (c + 1) * ZHEADS)
        def _(h):
            temporal_head(h)

    for s in range(SOURCES):
        dcv_own[s] = dot(bm[pl.ds(48, 16), :], dq5[1 + s].astype(BF16))
    dcv_x = (tm_peer, 4, lambda p: dcv_own.at[p], dcv, s_dcv, r_dcv, tm)
    start_all(*dcv_x)
    sent_all(*ctv_x)
    dcv[tm] = dcv_own[tm]
    dq_t = dq5[0].astype(BF16)
    dcodes_tq = dot(bm[pl.ds(32, 16), :], dq_t)
    grad_b = [dot(codes_tq, dq_t, NT)]
    part_v = dot(ctv[0], dq5[1].astype(BF16), NT)
    for s in range(1, SOURCES):
        part_v = part_v + dot(ctv[s], dq5[1 + s].astype(BF16), NT)
    grad_b.append(part_v)
    copy(kv.at[tm], kv.at[tm], s_z, r_z.at[0], (dp, across, sp)).wait_send()
    own_to_sibling.wait_send()
    copy(kv.at[across], kv.at[across], s_fwd, r_fwd.at[0], (dp, sibling, sp)).wait_send()
    received_all(*dcv_x)
    dcodes_tv = dcv[0] + dcv[1] + dcv[2] + dcv[3]
    dcodes_t = jnp.concatenate([dcodes_tq, dcodes_tv], axis=0).astype(BF16)
    dct_own[...] = dcodes_t
    dct_x = (space_peer, 16, lambda p: dct_own, dct_all, s_dct, r_dct, sp)
    start_all(*dct_x)
    dct_all[sp] = dcodes_t

    grad_a = dot(dcodes_t, ht[...].astype(BF16), NT)
    halves = [grad_a, jnp.concatenate(grad_b, axis=0)]
    for r in range(2):
        for c in range(9):
            gt_send[9 * r + c] = halves[r][:, 128 * c : 128 * (c + 1)].astype(BF16)
    gt_x = (block_peer, 32, lambda p: gt_send.at[p], gt_recv, s_gt, r_gt, block, PIECES)
    start_all(*gt_x)

    for i in range(D // 128):
        cols = pl.ds(i * 128, 128)
        mixed[:, cols] = t0[cols, :].T.astype(BF16)

    sent_all(*dcv_x)
    received_all(*dct_x)

    @pl.loop(0, 8)
    def _(j):
        lanes = pl.ds(pl.multiple_of(j * 128, 128), 128)
        even, odd = 2 * j, 2 * j + 1
        codes = to_frames(dct_all[even].astype(F32), dct_all[odd].astype(F32))
        for f in range(2):
            gf[f, :, lanes] = (
                cf[f, :, lanes] + dot(ah[pl.ds(32, 32), :], codes[f].astype(BF16), TN)
            ).astype(BF16)

    dv[...] = jnp.zeros_like(dv)

    def backward(f):
        @pl.loop(0, LENGTH // CHUNK)
        def _(i):
            lanes = pl.ds(pl.multiple_of(i * CHUNK, CHUNK), CHUNK)
            g = gf[f, :, lanes]
            inner = jnp.sum(g.astype(F32) * oe[f, :, lanes], axis=0, keepdims=True)
            dprob = dot(vn[f], g)
            dscore = (probs[f, :, lanes] * (dprob - inner)).astype(BF16)
            dq[f, :, lanes] = dot(kt[f], dscore)
            dv[f] += dot(g, probs_low[f, :, lanes], NT)

    def sum_slots(ref, count):
        total = ref[0].astype(F32)
        for k in range(1, count):
            total = total + ref[k].astype(F32)
        return total

    backward(0)
    z_t_x = (z_peer, 16, lambda p: z_t.at[z], z_t, s_zt, r_zt, z)

    @pl.when(block < PIECES)
    def _():
        gt_recv[block] = gt_send[block]
        received_all(block_peer, 32, lambda p: gt_send.at[p], gt_recv, s_gt, r_gt, block)
        z_t[z] = sum_slots(gt_recv, 32).astype(BF16)
        start_all(*z_t_x)

    backward(1)
    pad = jnp.zeros((128 - HEAD_DIM, LENGTH), F32)
    gb_q = jnp.zeros((16, 128), F32)
    gb_v = jnp.zeros((16, 128), F32)
    for f in range(2):
        dctf[f, pl.ds(0, 16), :] = dot(bh[pl.ds(0, 16), :], dq[f].astype(BF16))
        dctf[f, pl.ds(16, 16), :] = dot(bh[pl.ds(16, 16), :], dv[f].astype(BF16))

    @pl.loop(0, 8)
    def _(j):
        lanes = pl.ds(pl.multiple_of(j * 128, 128), 128)
        pair = from_frames(dctf[0, :, lanes], dctf[1, :, lanes])
        dcs_send[2 * j] = pair[0].astype(BF16)
        dcs_send[2 * j + 1] = pair[1].astype(BF16)

    dcs_x = (space_peer, 16, lambda p: dcs_send.at[p], dcs_recv, s_dcs, r_dcs, sp)
    start_all(*dcs_x)
    dcs_recv[sp] = dcs_send[sp]
    for f in range(2):
        dq_f = jnp.concatenate([dq[f], pad], axis=0).astype(BF16)
        dv_f = jnp.concatenate([dv[f], pad], axis=0).astype(BF16)
        gb_q = gb_q + dot(cc[f, pl.ds(0, 16), :], dq_f, NT)
        gb_v = gb_v + dot(cc[f, pl.ds(16, 16), :], dv_f, NT)
    gb_send[0] = gb_q.astype(BF16)
    gb_send[1] = gb_v.astype(BF16)
    to_sibling = copy(gb_send.at[1 - core], gb_recv, s_gb, r_gb, (dp, sibling, sp))
    to_sibling.start()
    sent_all(*dct_x)
    sent_all(*gt_x)
    received_all(*dcs_x)
    dcodes_s = sum_slots(dcs_recv, 16).astype(BF16)
    grad_s = dot(dcodes_s, patches[...])
    for r in range(2):
        for c in range(9):
            gs_send[9 * r + c] = grad_s[16 * r : 16 * (r + 1), 128 * c : 128 * (c + 1)].astype(BF16)
    gs_x = (block_peer, 32, lambda p: gs_send.at[p], gs_recv, s_gs, r_gs, block, PIECES)
    start_all(*gs_x)
    sent_all(*dcs_x)
    to_sibling.wait_recv()
    z_s[z, pl.ds(16, 16), :] = (gb_send[core].astype(F32) + gb_recv[...].astype(F32)).astype(BF16)

    @pl.when(block < PIECES)
    def _():
        received_all(*z_t_x)
        ag_t[block] = sum_slots(z_t, 16).astype(BF16)
        gs_recv[block] = gs_send[block]
        received_all(block_peer, 32, lambda p: gs_send.at[p], gs_recv, s_gs, r_gs, block)
        z_s[z, pl.ds(0, 16), :] = sum_slots(gs_recv, 32).astype(BF16)

    @pl.when(block >= PIECES)
    def _():
        z_s[z, pl.ds(0, 16), :] = jnp.zeros((16, 128), BF16)

    z_s_x = (z_peer, 16, lambda p: z_s.at[z], z_s, s_zs, r_zs, z)
    start_all(*z_s_x)
    ag_t_x = (block_peer, 32, lambda p: ag_t.at[block], ag_t, s_agt, r_agt, block)

    @pl.when(block < PIECES)
    def _():
        start_all(*ag_t_x)
        sent_all(*z_t_x)

    sent_all(*gs_x)
    to_sibling.wait_send()
    received_all(*ag_t_x, PIECES)
    for piece in range(PIECES):
        out = (ga, gb)[piece // 9]
        out[pl.ds(32, 32), pl.ds(128 * (piece % 9), 128)] = ag_t[piece]

    @pl.when(block < PIECES)
    def _():
        sent_all(*ag_t_x)

    received_all(*z_s_x)
    ag_s[block] = sum_slots(z_s, 16).astype(BF16)
    ag_s_x = (block_peer, 32, lambda p: ag_s.at[block], ag_s, s_ags, r_ags, block)
    start_all(*ag_s_x)
    sent_all(*z_s_x)
    received_all(*ag_s_x)
    for piece in range(PIECES):
        rows = pl.ds(16 * (piece // 9), 16)
        ga[rows, pl.ds(128 * (piece % 9), 128)] = ag_s[piece, pl.ds(0, 16), :]
    for r in range(2):
        tiles = [jnp.zeros((16, 128), F32) for _ in range(D // 128)]
        for h in range(HEADS):
            first, offset = divmod(h * HEAD_DIM, 128)
            piece = ag_s[2 * h + r, pl.ds(16, 16), :].astype(F32)
            if offset:
                piece = pltpu.roll(piece, offset, 1)
            lane = lax.broadcasted_iota(jnp.int32, (1, 128), 1)
            tiles[first] = tiles[first] + jnp.where(lane >= offset, piece, 0.0)
            if offset + HEAD_DIM > 128:
                tiles[first + 1] = tiles[first + 1] + jnp.where(lane < offset, piece, 0.0)
        for i in range(D // 128):
            gb[pl.ds(16 * r, 16), pl.ds(128 * i, 128)] = tiles[i].astype(BF16)
    sent_all(*ag_s_x)


def scratch():
    def f32(*shape):
        return pltpu.VMEM(shape, F32)

    def bf16(*shape):
        return pltpu.VMEM(shape, BF16)

    def sems(*shape):
        return pltpu.SemaphoreType.DMA(shape)

    whole = f32(D, TOK)
    one = pltpu.SemaphoreType.DMA
    return [
        *[bf16(TOK, D)] * 8, bf16(64, D), bf16(64, D), sems(10),
        bf16(64, HEAD_DIM), bf16(64, HEAD_DIM), f32(D, 64),
        whole, whole, whole, whole, whole, whole, f32(SOURCES, D, TOK), f32(1 + SOURCES, D, TOK),
        bf16(HEADS, 144, TOK), bf16(HEADS, 144, TOK), bf16(HEADS, 80, TOK), bf16(HEADS, 80, TOK),
        bf16(HEADS, 80, TOK), bf16(HEADS, 80, TOK), bf16(HEADS, 32, TOK), bf16(32, TOK),
        bf16(2, HEAD_DIM, LENGTH), bf16(2, LENGTH, HEAD_DIM), bf16(2, HEAD_DIM, LENGTH), bf16(2, LENGTH, HEAD_DIM),
        bf16(2, HEAD_DIM, LENGTH), f32(2, HEAD_DIM, LENGTH), bf16(2, 32, LENGTH), f32(2, LENGTH, LENGTH),
        bf16(2, LENGTH, LENGTH), f32(2, HEAD_DIM, LENGTH), f32(2, HEAD_DIM, LENGTH),
        bf16(HEADS, 80, TOK), bf16(HEADS, 80, TOK),
        bf16(SOURCES, HEADS, 144, TOK), bf16(SOURCES, 16, TOK), f32(SOURCES, 16, TOK), f32(SOURCES, 16, TOK),
        bf16(32, TOK), bf16(HEADS, 32, TOK), f32(2, 32, LENGTH), bf16(2, HEAD_DIM, LENGTH),
        f32(2, HEAD_DIM, LENGTH), f32(2, HEAD_DIM, LENGTH), bf16(HEADS, 32, TOK), bf16(HEADS, 32, TOK),
        bf16(PIECES, 32, 128), bf16(32, 32, 128), bf16(16, 32, 128), bf16(32, 32, 128),
        bf16(PIECES, 16, 128), bf16(32, 16, 128), bf16(2, 16, 128), bf16(16, 128), bf16(16, 32, 128), bf16(32, 32, 128),
        sems(3), sems(3), one, one, one, one,
        one, sems(ZCHUNKS), one, one, one, sems(ZCHUNKS),
        one, one, one, one, one, one, one, one,
        one, one, one, one, one, one,
        one, one, one, one, one, one, one, one,
    ]


def hand_over(mixed, ga, gb, mixed_out, ga_out, gb_out):
    mixed_out[...] = mixed[...]
    ga_out[...] = ga[...].astype(F32) * FACTOR
    gb_out[...] = gb[...].astype(F32) * FACTOR


def per_device(
    patches, query_s, key_s, value_s, query_t, key_t, value_t, adapters_a, adapters_b, cotangent
):
    at = jnp.swapaxes(adapters_a, 1, 2).reshape(64, D)
    bm = adapters_b.reshape(64, D)
    tokens = [
        array.reshape(TOK, D)
        for array in (patches, query_s, key_s, value_s, query_t, key_t, value_t, cotangent)
    ]
    out_shape = (
        jax.ShapeDtypeStruct((TOK, D), BF16),
        jax.ShapeDtypeStruct((64, D), F32),
        jax.ShapeDtypeStruct((64, D), F32),
    )
    results = pl.pallas_call(
        kernel,
        out_shape=(
            jax.ShapeDtypeStruct((TOK, D), BF16),
            jax.ShapeDtypeStruct((64, D), BF16),
            jax.ShapeDtypeStruct((64, D), BF16),
        ),
        in_specs=[pl.BlockSpec(memory_space=pl.ANY)] * 10,
        out_specs=[pl.BlockSpec(memory_space=pltpu.VMEM)] * 3,
        scratch_shapes=scratch(),
        compiler_params=pltpu.CompilerParams(
            collective_id=0, has_side_effects=True, vmem_limit_bytes=56 * 1024 * 1024
        ),
    )(*tokens, at, bm)
    mixed, ga, gb = pl.pallas_call(
        hand_over,
        out_shape=out_shape,
        in_specs=[pl.BlockSpec(memory_space=pltpu.VMEM)] * 3,
        out_specs=[pl.BlockSpec(memory_space=pltpu.VMEM)] * 3,
    )(*results)
    grads_a = jnp.swapaxes(ga.reshape(4, 16, D), 1, 2)
    grads_b = gb.reshape(4, 16, D)
    return mixed.reshape(patches.shape), grads_a, grads_b


def solution(mesh):
    tokens = P("dp", "tm", "space", None)
    return jax.shard_map(
        per_device,
        mesh=mesh,
        in_specs=(tokens,) * 7 + (P(), P(), tokens),
        out_specs=(tokens, P(), P()),
        check_vma=False,
    )
```

```python
import math

import jax
import jax.numpy as jnp
from jax import lax
from jax.experimental import pallas as pl
from jax.experimental.pallas import tpu as pltpu
from jax.sharding import PartitionSpec as P

MESH = pl.DeviceIdType.MESH
F32 = jnp.float32
BF16 = jnp.bfloat16

HEAD_DIM = 72
HEADS = 16
D = HEADS * HEAD_DIM
TOK = 128
LENGTH = 1024
CHUNK = 1024
SOURCES = 4
ZCHUNKS = 8
ZHEADS = HEADS // ZCHUNKS
PIECES = 18
SCALE = HEAD_DIM ** -0.5
FACTOR = 65536 ** -0.5
LOG2E = math.log2(math.e)

NN = (((1,), (0,)), ((), ()))
NT = (((1,), (1,)), ((), ()))
TN = (((0,), (0,)), ((), ()))


def dot(a, b, dims=NN):
    return lax.dot_general(a, b, dims, preferred_element_type=F32)


def rounded(x):
    return x.astype(BF16).astype(F32)


def half_turn(x):
    return pltpu.roll(x, 64, 1)


def low_lanes():
    return lax.broadcasted_iota(jnp.int32, (1, TOK), 1) < 64


def to_frames(a, b):
    low = low_lanes()
    return jnp.where(low, a, half_turn(b)), jnp.where(low, half_turn(a), b)


def from_frames(first, second):
    low = low_lanes()
    return jnp.where(low, first, half_turn(second)), jnp.where(low, half_turn(first), second)


def head_rows(h):
    return pl.ds(pl.multiple_of(h * HEAD_DIM, 8), HEAD_DIM)


def kernel(
    patches_hbm, query_s_hbm, key_s_hbm, value_s_hbm, query_t_hbm, key_t_hbm, value_t_hbm, cot_hbm, at_hbm, bm_hbm,
    mixed, ga, gb,
    patches, query_s, key_s, value_s, query_t, key_t, value_t, cot, at, bm, s_load,
    ah, bh, abt, t0, t1, xt, qtt, cott, ht, lv, dq5,
    send_kq, recv_kq, send_v, recv_v, send_c, recv_c, codes_all, codes_own,
    kt, kn, vt, vn, qt, cf, cc, probs, probs_low, ot, oe,
    o_send, o_recv,
    kv, ctv, dcv, dcv_own,
    dct_own, dct_all, dctf, gf, dq, dv, dcs_send, dcs_recv,
    gt_send, gt_recv, z_t, ag_t,
    gs_send, gs_recv, gb_send, gb_recv, z_s, ag_s,
    s_in, r_in, s_code, r_code, s_o, r_o,
    s_z, r_z, s_sib, r_sib, s_fwd, r_fwd,
    s_ctv, r_ctv, s_dcv, r_dcv, s_dct, r_dct, s_dcs, r_dcs,
    s_gt, r_gt, s_zt, r_zt, s_agt, r_agt,
    s_gs, r_gs, s_gb, r_gb, s_zs, r_zs, s_ags, r_ags, r_agh,
):
    dp, tm, sp = lax.axis_index("dp"), lax.axis_index("tm"), lax.axis_index("space")
    z_hi, core = tm // 2, tm % 2
    z = z_hi * 8 + dp
    block = core * 16 + sp

    def space_peer(step):
        peer = (sp + step) % 16
        return peer, (dp, tm, peer)

    def tm_peer(step):
        peer = (tm + step) % 4
        return peer, (dp, peer, sp)

    def block_peer(step):
        peer = (block + step) % 32
        return peer, (dp, z_hi * 2 + peer // 16, peer % 16)

    def z_peer(step):
        peer = (z + step) % 16
        return peer, (peer % 8, (peer // 8) * 2 + core, sp)

    across = (tm + 2) % 4
    sibling = z_hi * 2 + 1 - core
    far = (1 - z_hi) * 2 + 1 - core

    def copy(src, dst, s_sem, r_sem, device):
        return pltpu.make_async_remote_copy(
            src_ref=src, dst_ref=dst, send_sem=s_sem, recv_sem=r_sem, device_id=device, device_id_type=MESH
        )

    def start_all(peer_of, count, src_of, dst, s_sem, r_sem, me, limit=None):
        if limit is None:
            @pl.loop(1, count)
            def _(step):
                peer, device = peer_of(step)
                copy(src_of(peer), dst.at[me], s_sem, r_sem, device).start()
        else:
            @pl.loop(0, limit)
            def _(step):
                peer = (me + step) % limit

                @pl.when(peer != me)
                def _():
                    device = (dp, z_hi * 2 + peer // 16, peer % 16)
                    copy(src_of(peer), dst.at[me], s_sem, r_sem, device).start()

    def sent_all(peer_of, count, src_of, dst, s_sem, r_sem, me, limit=None):
        def wait(slots):
            all_slots = dst.at[pl.ds(0, slots)]
            copy(all_slots, all_slots, s_sem, r_sem, peer_of(1)[1]).wait_send()

        if limit is None:
            wait(count - 1)
        else:
            pl.when(me < limit)(lambda: wait(limit - 1))
            pl.when(me >= limit)(lambda: wait(limit))

    def received_all(peer_of, count, src_of, dst, s_sem, r_sem, me, limit=None):
        def wait(slots):
            all_slots = dst.at[pl.ds(0, slots)]
            copy(all_slots, all_slots, s_sem, r_sem, peer_of(1)[1]).wait_recv()

        if limit is None:
            wait(count - 1)
        else:
            pl.when(me < limit)(lambda: wait(limit - 1))
            pl.when(me >= limit)(lambda: wait(limit))

    def sum_slots(ref, count):
        total = ref[0].astype(F32)
        for k in range(1, count):
            total = total + ref[k].astype(F32)
        return total

    barrier = pltpu.get_barrier_semaphore()
    pl.semaphore_signal(barrier, inc=1, device_id=(dp, far, sp), device_id_type=MESH)

    @pl.loop(1, 16)
    def _(step):
        pl.semaphore_signal(barrier, inc=1, device_id=z_peer(step)[1], device_id_type=MESH)

    @pl.loop(1, 32)
    def _(step):
        pl.semaphore_signal(barrier, inc=1, device_id=block_peer(step)[1], device_id_type=MESH)

    loads = {}
    for i, (src, dst) in enumerate((
        (key_t_hbm, key_t), (value_t_hbm, value_t), (patches_hbm, patches), (at_hbm, at), (key_s_hbm, key_s),
        (query_s_hbm, query_s), (value_s_hbm, value_s), (cot_hbm, cot), (bm_hbm, bm), (query_t_hbm, query_t),
    )):
        loads[id(dst)] = pltpu.make_async_copy(src, dst, s_load.at[i])
        loads[id(dst)].start()

    def transpose_in(src, dst):
        loads[id(src)].wait()
        for i in range(D // 128):
            dst[pl.ds(i * 128, 128), :] = src[:, pl.ds(i * 128, 128)].astype(F32).T

    transpose_in(key_t, t0)
    transpose_in(value_t, t1)

    @pl.loop(0, HEADS)
    def _(h):
        rows = head_rows(h)
        kv[tm, h] = jnp.concatenate([t0[rows, :], t1[rows, :]], axis=0).astype(BF16)

    loads[id(patches)].wait()
    loads[id(at)].wait()
    codes_own[...] = dot(at[pl.ds(0, 32), :], patches[...], NT).astype(BF16)
    transpose_in(key_s, t0)
    transpose_in(query_s, t1)

    @pl.loop(0, HEADS)
    def _(h):
        rows = head_rows(h)
        send_kq[h] = jnp.concatenate([t0[rows, :], t1[rows, :]], axis=0).astype(BF16)

    pl.semaphore_wait(barrier, 1 + 15 + 31)

    def z_slot(source, c):
        return kv.at[source, pl.ds(c * ZHEADS, ZHEADS)]

    def send_chunk(c):
        copy(z_slot(tm, c), z_slot(tm, c), s_z, r_z.at[c], (dp, across, sp)).start()

    for c in range(ZCHUNKS):
        send_chunk(c)
    codes_x = (space_peer, 16, lambda p: codes_own, codes_all, s_code, r_code, sp)
    start_all(*codes_x)
    kq_x = (space_peer, 16, lambda p: send_kq.at[p], recv_kq, s_in.at[0], r_in.at[0], sp)
    v_x = (space_peer, 16, lambda p: send_v.at[p], recv_v, s_in.at[1], r_in.at[1], sp)
    c_x = (space_peer, 16, lambda p: send_c.at[p], recv_c, s_in.at[2], r_in.at[2], sp)
    start_all(*kq_x)
    own_to_sibling = copy(kv.at[tm], kv.at[tm], s_sib, r_sib, (dp, sibling, sp))
    own_to_sibling.start()
    gap = jnp.zeros((8, TOK), F32)

    def pack(src, dst):
        @pl.loop(0, HEADS)
        def _(h):
            dst[h] = jnp.concatenate([src[head_rows(h), :], gap], axis=0).astype(BF16)

    transpose_in(value_s, t0)
    pack(t0, send_v)
    start_all(*v_x)
    transpose_in(cot, cott)
    pack(cott, send_c)
    recv_kq[sp] = send_kq[sp]
    recv_v[sp] = send_v[sp]
    recv_c[sp] = send_c[sp]
    codes_all[sp] = codes_own[...]
    for i in range(D // 128):
        xt[pl.ds(i * 128, 128), :] = patches[:, pl.ds(i * 128, 128)].astype(F32).T
    transpose_in(query_t, qtt)
    loads[id(bm)].wait()
    for src, dst in ((at, ah), (bm, bh)):
        for i in range(D // 128):
            abt[pl.ds(i * 128, 128), :] = src[:, pl.ds(i * 128, 128)].astype(F32).T
        dst[...] = abt[head_rows(sp), :].T.astype(BF16)

    received_all(*codes_x)
    received_all(*kq_x)
    received_all(*v_x)

    @pl.loop(0, 8)
    def _(j):
        lanes = pl.ds(pl.multiple_of(j * 128, 128), 128)
        even, odd = 2 * j, 2 * j + 1
        kq = to_frames(recv_kq[even].astype(F32), recv_kq[odd].astype(F32))
        value = to_frames(recv_v[even].astype(F32), recv_v[odd].astype(F32))
        codes = to_frames(codes_all[even].astype(F32), codes_all[odd].astype(F32))
        for f in range(2):
            code = codes[f].astype(BF16)
            cc[f, :, lanes] = code
            keys = kq[f][:HEAD_DIM]
            query = kq[f][HEAD_DIM:] + dot(bh[pl.ds(0, 16), :], code[:16], TN)
            values = rounded(value[f][:HEAD_DIM] + dot(bh[pl.ds(16, 16), :], code[16:], TN))
            kt[f, :, lanes] = keys.astype(BF16)
            kn[f, lanes, :] = keys.T.astype(BF16)
            qt[f, :, lanes] = query.astype(BF16)
            vt[f, :, lanes] = values.astype(BF16)
            vn[f, lanes, :] = values.T.astype(BF16)

    def forward(f):
        @pl.loop(0, LENGTH // CHUNK)
        def _(i):
            lanes = pl.ds(pl.multiple_of(i * CHUNK, CHUNK), CHUNK)
            scores = dot(kn[f], qt[f, :, lanes])
            weights = jnp.exp2((scores - jnp.max(scores, axis=0, keepdims=True)) * (SCALE * LOG2E))
            p = weights * (1.0 / jnp.sum(weights, axis=0, keepdims=True))
            low = p.astype(BF16)
            probs[f, :, lanes] = p * SCALE
            probs_low[f, :, lanes] = low
            out = dot(vt[f], low)
            ot[f, :, lanes] = out
            oe[f, :, lanes] = out + dot(vt[f], (p - low.astype(F32)).astype(BF16))

    forward(0)
    forward(1)

    @pl.loop(0, 8)
    def _(j):
        lanes = pl.ds(pl.multiple_of(j * 128, 128), 128)
        pair = from_frames(ot[0, :, lanes], ot[1, :, lanes])
        for k in range(2):
            o_send[2 * j + k] = jnp.concatenate([pair[k], jnp.zeros((8, TOK), F32)], axis=0).astype(BF16)

    o_x = (space_peer, 16, lambda p: o_send.at[p], o_recv, s_o, r_o, sp)
    start_all(*o_x)
    o_recv[sp] = o_send[sp]
    sent_all(*codes_x)
    sent_all(*kq_x)
    sent_all(*v_x)
    received_all(*o_x)
    start_all(*c_x)

    @pl.loop(0, HEADS)
    def _(h):
        rows = head_rows(h)
        ht[rows, :] = rounded(xt[rows, :] + o_recv[h].astype(F32)[:HEAD_DIM])

    hidden = ht[...].astype(BF16)
    codes_t = dot(at[pl.ds(32, 32), :], hidden).astype(BF16)
    codes_tq = codes_t[:16]
    ctv[tm] = codes_t[16:]
    ctv_x = (tm_peer, 4, lambda p: ctv.at[tm], ctv, s_ctv, r_ctv, tm)
    start_all(*ctv_x)
    sent_all(*o_x)
    qtt[...] = rounded(qtt[...] + dot(bm[pl.ds(32, 16), :], codes_tq, TN))
    received_all(*ctv_x)
    for s in range(SOURCES):
        lv[s] = dot(bm[pl.ds(48, 16), :], ctv[s], TN)

    def temporal_head(h):
        rows = head_rows(h)
        q, g = qtt[rows, :], cott[rows, :]
        keys, values, straight, turned, d_straight, d_turned = [], [], [], [], [], []
        for s in range(SOURCES):
            both = kv[s, h].astype(F32)
            k, v = both[:HEAD_DIM], rounded(both[HEAD_DIM:] + lv[s, rows, :])
            k_r, v_r = half_turn(k), half_turn(v)
            keys.append((k, k_r))
            values.append((v, v_r))
            straight.append(jnp.sum(q * k, axis=0, keepdims=True))
            turned.append(jnp.sum(q * k_r, axis=0, keepdims=True))
            d_straight.append(jnp.sum(g * v, axis=0, keepdims=True))
            d_turned.append(jnp.sum(g * v_r, axis=0, keepdims=True))
        scores = jnp.concatenate(straight + turned, axis=0)
        weights = jnp.exp2((scores - jnp.max(scores, axis=0, keepdims=True)) * (SCALE * LOG2E))
        p = weights * (1.0 / jnp.sum(weights, axis=0, keepdims=True))
        dprob = jnp.concatenate(d_straight + d_turned, axis=0)
        inner = jnp.sum(p * dprob, axis=0, keepdims=True)
        dscore = rounded(p * (dprob - inner) * SCALE)
        low = rounded(p)
        low_r, g_r = half_turn(low), half_turn(g)
        out = jnp.zeros((HEAD_DIM, TOK), F32)
        dquery = jnp.zeros((HEAD_DIM, TOK), F32)
        for s in range(SOURCES):
            out = out + low[s : s + 1] * values[s][0] + low[s + 4 : s + 5] * values[s][1]
            dquery = dquery + dscore[s : s + 1] * keys[s][0] + dscore[s + 4 : s + 5] * keys[s][1]
            dq5[1 + s, rows, :] = low[s : s + 1] * g + low_r[s + 4 : s + 5] * g_r
        dq5[0, rows, :] = dquery
        t0[rows, :] = ht[rows, :] + rounded(out)

    own_to_sibling.wait_recv()

    def relay_chunk(c):
        copy(z_slot(tm, c), z_slot(across, c), s_z, r_z.at[c], (dp, across, sp)).wait_recv()
        copy(z_slot(across, c), z_slot(across, c), s_fwd, r_fwd.at[c], (dp, sibling, sp)).start()

    sent_all(*c_x)
    received_all(*c_x)

    @pl.loop(0, 8)
    def _(j):
        lanes = pl.ds(pl.multiple_of(j * 128, 128), 128)
        even, odd = 2 * j, 2 * j + 1
        grad = to_frames(recv_c[even].astype(F32), recv_c[odd].astype(F32))
        for f in range(2):
            cf[f, :, lanes] = grad[f][:HEAD_DIM]

    relay_chunk(0)
    for c in range(ZCHUNKS):
        if c + 1 < ZCHUNKS:
            relay_chunk(c + 1)
        copy(z_slot(across, c), z_slot(far, c), s_fwd, r_fwd.at[c], (dp, sibling, sp)).wait_recv()

        @pl.loop(c * ZHEADS, (c + 1) * ZHEADS)
        def _(h):
            temporal_head(h)

    for s in range(SOURCES):
        dcv_own[s] = dot(bm[pl.ds(48, 16), :], dq5[1 + s].astype(BF16)).astype(BF16)
    dcv_x = (tm_peer, 4, lambda p: dcv_own.at[p], dcv, s_dcv, r_dcv, tm)
    start_all(*dcv_x)
    sent_all(*ctv_x)
    dcv[tm] = dcv_own[tm]
    dq_t = dq5[0].astype(BF16)
    dcodes_tq = dot(bm[pl.ds(32, 16), :], dq_t)
    grad_b = [dot(codes_tq, dq_t, NT)]
    part_v = dot(ctv[0], dq5[1].astype(BF16), NT)
    for s in range(1, SOURCES):
        part_v = part_v + dot(ctv[s], dq5[1 + s].astype(BF16), NT)
    grad_b.append(part_v)
    copy(kv.at[tm], kv.at[tm], s_z, r_z.at[0], (dp, across, sp)).wait_send()
    own_to_sibling.wait_send()
    copy(kv.at[across], kv.at[across], s_fwd, r_fwd.at[0], (dp, sibling, sp)).wait_send()
    received_all(*dcv_x)
    dcodes_tv = sum_slots(dcv, SOURCES)
    dcodes_t = jnp.concatenate([dcodes_tq, dcodes_tv], axis=0).astype(BF16)
    dct_own[...] = dcodes_t
    dct_x = (space_peer, 16, lambda p: dct_own, dct_all, s_dct, r_dct, sp)
    start_all(*dct_x)
    dct_all[sp] = dcodes_t

    grad_a = dot(dcodes_t, ht[...].astype(BF16), NT)
    halves = [grad_a, jnp.concatenate(grad_b, axis=0)]
    for r in range(2):
        for c in range(9):
            gt_send[9 * r + c] = halves[r][:, 128 * c : 128 * (c + 1)].astype(BF16)
    gt_x = (block_peer, 32, lambda p: gt_send.at[p], gt_recv, s_gt, r_gt, block, PIECES)
    start_all(*gt_x)

    for i in range(D // 128):
        cols = pl.ds(i * 128, 128)
        mixed[:, cols] = t0[cols, :].T.astype(BF16)

    sent_all(*dcv_x)
    received_all(*dct_x)

    @pl.loop(0, 8)
    def _(j):
        lanes = pl.ds(pl.multiple_of(j * 128, 128), 128)
        even, odd = 2 * j, 2 * j + 1
        codes = to_frames(dct_all[even].astype(F32), dct_all[odd].astype(F32))
        for f in range(2):
            gf[f, :, lanes] = (
                cf[f, :, lanes] + dot(ah[pl.ds(32, 32), :], codes[f].astype(BF16), TN)
            ).astype(BF16)

    dv[...] = jnp.zeros_like(dv)

    def backward(f):
        @pl.loop(0, LENGTH // CHUNK)
        def _(i):
            lanes = pl.ds(pl.multiple_of(i * CHUNK, CHUNK), CHUNK)
            g = gf[f, :, lanes]
            inner = jnp.sum(g.astype(F32) * oe[f, :, lanes], axis=0, keepdims=True)
            dprob = dot(vn[f], g)
            dscore = (probs[f, :, lanes] * (dprob - inner)).astype(BF16)
            dq[f, :, lanes] = dot(kt[f], dscore)
            dv[f] += dot(g, probs_low[f, :, lanes], NT)

    backward(0)
    z_t_x = (z_peer, 16, lambda p: z_t.at[z], z_t, s_zt, r_zt, z)

    @pl.when(block < PIECES)
    def _():
        gt_recv[block] = gt_send[block]
        received_all(block_peer, 32, lambda p: gt_send.at[p], gt_recv, s_gt, r_gt, block)
        z_t[z] = sum_slots(gt_recv, 32).astype(BF16)
        start_all(*z_t_x)

    backward(1)
    pad = jnp.zeros((128 - HEAD_DIM, LENGTH), F32)
    gb_q = jnp.zeros((16, 128), F32)
    gb_v = jnp.zeros((16, 128), F32)
    for f in range(2):
        dctf[f, pl.ds(0, 16), :] = dot(bh[pl.ds(0, 16), :], dq[f].astype(BF16))
        dctf[f, pl.ds(16, 16), :] = dot(bh[pl.ds(16, 16), :], dv[f].astype(BF16))

    @pl.loop(0, 8)
    def _(j):
        lanes = pl.ds(pl.multiple_of(j * 128, 128), 128)
        pair = from_frames(dctf[0, :, lanes], dctf[1, :, lanes])
        dcs_send[2 * j] = pair[0].astype(BF16)
        dcs_send[2 * j + 1] = pair[1].astype(BF16)

    dcs_x = (space_peer, 16, lambda p: dcs_send.at[p], dcs_recv, s_dcs, r_dcs, sp)
    start_all(*dcs_x)
    dcs_recv[sp] = dcs_send[sp]
    for f in range(2):
        dq_f = jnp.concatenate([dq[f], pad], axis=0).astype(BF16)
        dv_f = jnp.concatenate([dv[f], pad], axis=0).astype(BF16)
        gb_q = gb_q + dot(cc[f, pl.ds(0, 16), :], dq_f, NT)
        gb_v = gb_v + dot(cc[f, pl.ds(16, 16), :], dv_f, NT)
    gb_send[0] = gb_q.astype(BF16)
    gb_send[1] = gb_v.astype(BF16)
    to_sibling = copy(gb_send.at[1 - core], gb_recv, s_gb, r_gb, (dp, sibling, sp))
    to_sibling.start()
    sent_all(*dct_x)
    sent_all(*gt_x)
    received_all(*dcs_x)
    dcodes_s = sum_slots(dcs_recv, 16).astype(BF16)
    grad_s = dot(dcodes_s, patches[...])
    for r in range(2):
        for c in range(9):
            gs_send[9 * r + c] = grad_s[16 * r : 16 * (r + 1), 128 * c : 128 * (c + 1)].astype(BF16)
    gs_x = (block_peer, 32, lambda p: gs_send.at[p], gs_recv, s_gs, r_gs, block, PIECES)
    start_all(*gs_x)
    sent_all(*dcs_x)
    to_sibling.wait_recv()
    z_s[z, pl.ds(16, 16), :] = (gb_send[core].astype(F32) + gb_recv[...].astype(F32)).astype(BF16)

    @pl.when(block < PIECES)
    def _():
        received_all(*z_t_x)
        ag_t[block] = sum_slots(z_t, 16).astype(BF16)
        gs_recv[block] = gs_send[block]
        received_all(block_peer, 32, lambda p: gs_send.at[p], gs_recv, s_gs, r_gs, block)
        z_s[z, pl.ds(0, 16), :] = sum_slots(gs_recv, 32).astype(BF16)

    z_half = z_s.at[pl.ds(0, 16), pl.ds(16, 16)]
    z_s_x = (z_peer, 16, lambda p: z_s.at[z], z_s, s_zs, r_zs, z)
    z_h_x = (z_peer, 16, lambda p: z_half.at[z], z_half, s_zs, r_zs, z)
    has_piece = pl.when(block < PIECES)
    no_piece = pl.when(block >= PIECES)
    has_piece(lambda: start_all(*z_s_x))
    no_piece(lambda: start_all(*z_h_x))
    ag_t_x = (block_peer, 32, lambda p: ag_t.at[block], ag_t, s_agt, r_agt, block)

    @pl.when(block < PIECES)
    def _():
        start_all(*ag_t_x)
        sent_all(*z_t_x)

    sent_all(*gs_x)
    to_sibling.wait_send()
    received_all(*ag_t_x, PIECES)
    for piece in range(PIECES):
        out = (ga, gb)[piece // 9]
        out[pl.ds(32, 32), pl.ds(128 * (piece % 9), 128)] = ag_t[piece]

    @pl.when(block < PIECES)
    def _():
        sent_all(*ag_t_x)

    ag_half = ag_s.at[pl.ds(0, 32), pl.ds(16, 16)]
    ag_s_x = (block_peer, 32, lambda p: ag_s.at[block], ag_s, s_ags, r_ags, block)
    ag_h_x = (block_peer, 32, lambda p: ag_half.at[block], ag_half, s_ags, r_agh, block)

    @has_piece
    def _():
        received_all(*z_s_x)
        ag_s[block] = sum_slots(z_s, 16).astype(BF16)
        start_all(*ag_s_x)
        sent_all(*z_s_x)
        received_all(*ag_s_x, PIECES)
        everything = ag_half.at[pl.ds(0, 32 - PIECES)]
        copy(everything, everything, s_ags, r_agh, (dp, sibling, sp)).wait_recv()

    @no_piece
    def _():
        received_all(*z_h_x)
        total = z_s[0, pl.ds(16, 16), :].astype(F32)
        for k in range(1, 16):
            total = total + z_s[k, pl.ds(16, 16), :].astype(F32)
        ag_s[block, pl.ds(16, 16), :] = total.astype(BF16)
        start_all(*ag_h_x)
        sent_all(*z_h_x)
        received_all(*ag_s_x, PIECES)
        others = ag_half.at[pl.ds(0, 31 - PIECES)]
        copy(others, others, s_ags, r_agh, (dp, sibling, sp)).wait_recv()

    for piece in range(PIECES):
        rows = pl.ds(16 * (piece // 9), 16)
        ga[rows, pl.ds(128 * (piece % 9), 128)] = ag_s[piece, pl.ds(0, 16), :]
    for r in range(2):
        tiles = [jnp.zeros((16, 128), F32) for _ in range(D // 128)]
        for h in range(HEADS):
            first, offset = divmod(h * HEAD_DIM, 128)
            piece = ag_s[16 * r + h, pl.ds(16, 16), :].astype(F32)
            if offset:
                piece = pltpu.roll(piece, offset, 1)
            lane = lax.broadcasted_iota(jnp.int32, (1, 128), 1)
            tiles[first] = tiles[first] + jnp.where(lane >= offset, piece, 0.0)
            if offset + HEAD_DIM > 128:
                tiles[first + 1] = tiles[first + 1] + jnp.where(lane < offset, piece, 0.0)
        for i in range(D // 128):
            gb[pl.ds(16 * r, 16), pl.ds(128 * i, 128)] = tiles[i].astype(BF16)
    has_piece(lambda: sent_all(*ag_s_x))
    no_piece(lambda: sent_all(*ag_h_x))


def scratch():
    def f32(*shape):
        return pltpu.VMEM(shape, F32)

    def bf16(*shape):
        return pltpu.VMEM(shape, BF16)

    def sems(*shape):
        return pltpu.SemaphoreType.DMA(shape)

    whole = f32(D, TOK)
    one = pltpu.SemaphoreType.DMA
    return [
        *[bf16(TOK, D)] * 8, bf16(64, D), bf16(64, D), sems(10),
        bf16(64, HEAD_DIM), bf16(64, HEAD_DIM), f32(D, 64),
        whole, whole, whole, whole, whole, whole, f32(SOURCES, D, TOK), f32(1 + SOURCES, D, TOK),
        bf16(HEADS, 144, TOK), bf16(HEADS, 144, TOK), bf16(HEADS, 80, TOK), bf16(HEADS, 80, TOK),
        bf16(HEADS, 80, TOK), bf16(HEADS, 80, TOK), bf16(HEADS, 32, TOK), bf16(32, TOK),
        bf16(2, HEAD_DIM, LENGTH), bf16(2, LENGTH, HEAD_DIM), bf16(2, HEAD_DIM, LENGTH), bf16(2, LENGTH, HEAD_DIM),
        bf16(2, HEAD_DIM, LENGTH), f32(2, HEAD_DIM, LENGTH), bf16(2, 32, LENGTH), f32(2, LENGTH, LENGTH),
        bf16(2, LENGTH, LENGTH), f32(2, HEAD_DIM, LENGTH), f32(2, HEAD_DIM, LENGTH),
        bf16(HEADS, 80, TOK), bf16(HEADS, 80, TOK),
        bf16(SOURCES, HEADS, 144, TOK), bf16(SOURCES, 16, TOK), bf16(SOURCES, 16, TOK), bf16(SOURCES, 16, TOK),
        bf16(32, TOK), bf16(HEADS, 32, TOK), f32(2, 32, LENGTH), bf16(2, HEAD_DIM, LENGTH),
        f32(2, HEAD_DIM, LENGTH), f32(2, HEAD_DIM, LENGTH), bf16(HEADS, 32, TOK), bf16(HEADS, 32, TOK),
        bf16(PIECES, 32, 128), bf16(32, 32, 128), bf16(16, 32, 128), bf16(32, 32, 128),
        bf16(PIECES, 16, 128), bf16(32, 16, 128), bf16(2, 16, 128), bf16(16, 128), bf16(16, 32, 128), bf16(32, 32, 128),
        sems(3), sems(3), one, one, one, one,
        one, sems(ZCHUNKS), one, one, one, sems(ZCHUNKS),
        one, one, one, one, one, one, one, one,
        one, one, one, one, one, one,
        one, one, one, one, one, one, one, one, one,
    ]


def hand_over(mixed, ga, gb, mixed_out, ga_out, gb_out):
    mixed_out[...] = mixed[...]
    ga_out[...] = ga[...].astype(F32) * FACTOR
    gb_out[...] = gb[...].astype(F32) * FACTOR


def per_device(
    patches, query_s, key_s, value_s, query_t, key_t, value_t, adapters_a, adapters_b, cotangent
):
    at = jnp.swapaxes(adapters_a, 1, 2).reshape(64, D)
    bm = adapters_b.reshape(64, D)
    tokens = [
        array.reshape(TOK, D)
        for array in (patches, query_s, key_s, value_s, query_t, key_t, value_t, cotangent)
    ]
    out_shape = (
        jax.ShapeDtypeStruct((TOK, D), BF16),
        jax.ShapeDtypeStruct((64, D), F32),
        jax.ShapeDtypeStruct((64, D), F32),
    )
    results = pl.pallas_call(
        kernel,
        out_shape=(
            jax.ShapeDtypeStruct((TOK, D), BF16),
            jax.ShapeDtypeStruct((64, D), BF16),
            jax.ShapeDtypeStruct((64, D), BF16),
        ),
        in_specs=[pl.BlockSpec(memory_space=pl.ANY)] * 10,
        out_specs=[pl.BlockSpec(memory_space=pltpu.VMEM)] * 3,
        scratch_shapes=scratch(),
        compiler_params=pltpu.CompilerParams(
            collective_id=0, has_side_effects=True, vmem_limit_bytes=56 * 1024 * 1024
        ),
    )(*tokens, at, bm)
    mixed, ga, gb = pl.pallas_call(
        hand_over,
        out_shape=out_shape,
        in_specs=[pl.BlockSpec(memory_space=pltpu.VMEM)] * 3,
        out_specs=[pl.BlockSpec(memory_space=pltpu.VMEM)] * 3,
    )(*results)
    grads_a = jnp.swapaxes(ga.reshape(4, 16, D), 1, 2)
    grads_b = gb.reshape(4, 16, D)
    return mixed.reshape(patches.shape), grads_a, grads_b


def solution(mesh):
    tokens = P("dp", "tm", "space", None)
    return jax.shard_map(
        per_device,
        mesh=mesh,
        in_specs=(tokens,) * 7 + (P(), P(), tokens),
        out_specs=(tokens, P(), P()),
        check_vma=False,
    )
```

```python
import math

import jax
import jax.numpy as jnp
from jax import lax
from jax.experimental import pallas as pl
from jax.experimental.pallas import tpu as pltpu
from jax.sharding import PartitionSpec as P

MESH = pl.DeviceIdType.MESH
F32 = jnp.float32
BF16 = jnp.bfloat16

HEAD_DIM = 72
HEADS = 16
D = HEADS * HEAD_DIM
TOK = 128
LENGTH = 1024
CHUNK = 1024
SOURCES = 4
ZCHUNKS = 4
ZHEADS = HEADS // ZCHUNKS
PIECES = 18
SCALE = HEAD_DIM ** -0.5
FACTOR = 65536 ** -0.5
LOG2E = math.log2(math.e)

NN = (((1,), (0,)), ((), ()))
NT = (((1,), (1,)), ((), ()))
TN = (((0,), (0,)), ((), ()))


def dot(a, b, dims=NN):
    return lax.dot_general(a, b, dims, preferred_element_type=F32)


def rounded(x):
    return x.astype(BF16).astype(F32)


def half_turn(x):
    return pltpu.roll(x, 64, 1)


def low_lanes():
    return lax.broadcasted_iota(jnp.int32, (1, TOK), 1) < 64


def to_frames(a, b):
    low = low_lanes()
    return jnp.where(low, a, half_turn(b)), jnp.where(low, half_turn(a), b)


def from_frames(first, second):
    low = low_lanes()
    return jnp.where(low, first, half_turn(second)), jnp.where(low, half_turn(first), second)


def head_rows(h):
    return pl.ds(pl.multiple_of(h * HEAD_DIM, 8), HEAD_DIM)


def kernel(
    patches_hbm, query_s_hbm, key_s_hbm, value_s_hbm, query_t_hbm, key_t_hbm, value_t_hbm, cot_hbm, at_hbm, bm_hbm,
    mixed, ga, gb,
    patches, query_s, key_s, value_s, query_t, key_t, value_t, cot, at, bm, s_load,
    ah, bh, abt, t0, t1, xt, qtt, cott, ht, lv, dq5,
    send_kq, recv_kq, send_v, recv_v, send_c, recv_c, codes_all, codes_own,
    kt, kn, vt, vn, qt, cf, cc, probs, probs_low, ot, oe,
    o_send, o_recv,
    kv, ctv, dcv, dcv_own,
    dct_own, dct_all, dctf, gf, dq, dv, dcs_send, dcs_recv,
    gt_send, gt_recv, z_t, ag_t,
    gs_send, gs_recv, gb_send, gb_recv, z_s, ag_s,
    s_in, r_in, s_code, r_code, s_o, r_o,
    s_z, r_z, s_sib, r_sib, s_fwd, r_fwd,
    s_ctv, r_ctv, s_dcv, r_dcv, s_dct, r_dct, s_dcs, r_dcs,
    s_gt, r_gt, s_zt, r_zt, s_agt, r_agt,
    s_gs, r_gs, s_gb, r_gb, s_zs, r_zs, s_ags, r_ags, r_agh,
):
    dp, tm, sp = lax.axis_index("dp"), lax.axis_index("tm"), lax.axis_index("space")
    z_hi, core = tm // 2, tm % 2
    z = z_hi * 8 + dp
    block = core * 16 + sp

    def space_peer(step):
        peer = (sp + step) % 16
        return peer, (dp, tm, peer)

    def tm_peer(step):
        peer = (tm + step) % 4
        return peer, (dp, peer, sp)

    def block_peer(step):
        peer = (block + step) % 32
        return peer, (dp, z_hi * 2 + peer // 16, peer % 16)

    def z_peer(step):
        peer = (z + step) % 16
        return peer, (peer % 8, (peer // 8) * 2 + core, sp)

    across = (tm + 2) % 4
    sibling = z_hi * 2 + 1 - core
    far = (1 - z_hi) * 2 + 1 - core

    def copy(src, dst, s_sem, r_sem, device):
        return pltpu.make_async_remote_copy(
            src_ref=src, dst_ref=dst, send_sem=s_sem, recv_sem=r_sem, device_id=device, device_id_type=MESH
        )

    def start_all(peer_of, count, src_of, dst, s_sem, r_sem, me, limit=None):
        if limit is None:
            @pl.loop(1, count)
            def _(step):
                peer, device = peer_of(step)
                copy(src_of(peer), dst.at[me], s_sem, r_sem, device).start()
        else:
            @pl.loop(0, limit)
            def _(step):
                peer = (me + step) % limit

                @pl.when(peer != me)
                def _():
                    device = (dp, z_hi * 2 + peer // 16, peer % 16)
                    copy(src_of(peer), dst.at[me], s_sem, r_sem, device).start()

    def sent_all(peer_of, count, src_of, dst, s_sem, r_sem, me, limit=None):
        def wait(slots):
            all_slots = dst.at[pl.ds(0, slots)]
            copy(all_slots, all_slots, s_sem, r_sem, peer_of(1)[1]).wait_send()

        if limit is None:
            wait(count - 1)
        else:
            pl.when(me < limit)(lambda: wait(limit - 1))
            pl.when(me >= limit)(lambda: wait(limit))

    def received_all(peer_of, count, src_of, dst, s_sem, r_sem, me, limit=None):
        def wait(slots):
            all_slots = dst.at[pl.ds(0, slots)]
            copy(all_slots, all_slots, s_sem, r_sem, peer_of(1)[1]).wait_recv()

        if limit is None:
            wait(count - 1)
        else:
            pl.when(me < limit)(lambda: wait(limit - 1))
            pl.when(me >= limit)(lambda: wait(limit))

    def sum_slots(ref, count):
        total = ref[0].astype(F32)
        for k in range(1, count):
            total = total + ref[k].astype(F32)
        return total

    barrier = pltpu.get_barrier_semaphore()
    pl.semaphore_signal(barrier, inc=1, device_id=(dp, far, sp), device_id_type=MESH)

    @pl.loop(1, 16)
    def _(step):
        pl.semaphore_signal(barrier, inc=1, device_id=z_peer(step)[1], device_id_type=MESH)

    @pl.loop(1, 32)
    def _(step):
        pl.semaphore_signal(barrier, inc=1, device_id=block_peer(step)[1], device_id_type=MESH)

    loads = {}
    for i, (src, dst) in enumerate((
        (key_t_hbm, key_t), (value_t_hbm, value_t), (patches_hbm, patches), (at_hbm, at), (key_s_hbm, key_s),
        (query_s_hbm, query_s), (value_s_hbm, value_s), (cot_hbm, cot), (bm_hbm, bm), (query_t_hbm, query_t),
    )):
        loads[id(dst)] = pltpu.make_async_copy(src, dst, s_load.at[i])
        loads[id(dst)].start()

    def transpose_in(src, dst):
        loads[id(src)].wait()
        for i in range(D // 128):
            dst[pl.ds(i * 128, 128), :] = src[:, pl.ds(i * 128, 128)].astype(F32).T

    transpose_in(key_t, t0)
    transpose_in(value_t, t1)

    @pl.loop(0, HEADS)
    def _(h):
        rows = head_rows(h)
        kv[tm, h] = jnp.concatenate([t0[rows, :], t1[rows, :]], axis=0).astype(BF16)

    loads[id(patches)].wait()
    loads[id(at)].wait()
    codes_own[...] = dot(at[pl.ds(0, 32), :], patches[...], NT).astype(BF16)
    transpose_in(key_s, t0)
    transpose_in(query_s, t1)

    @pl.loop(0, HEADS)
    def _(h):
        rows = head_rows(h)
        send_kq[h] = jnp.concatenate([t0[rows, :], t1[rows, :]], axis=0).astype(BF16)

    pl.semaphore_wait(barrier, 1 + 15 + 31)

    def z_slot(source, c):
        return kv.at[source, pl.ds(c * ZHEADS, ZHEADS)]

    def send_chunk(c):
        copy(z_slot(tm, c), z_slot(tm, c), s_z, r_z.at[c], (dp, across, sp)).start()

    for c in range(ZCHUNKS):
        send_chunk(c)
    codes_x = (space_peer, 16, lambda p: codes_own, codes_all, s_code, r_code, sp)
    start_all(*codes_x)
    kq_x = (space_peer, 16, lambda p: send_kq.at[p], recv_kq, s_in.at[0], r_in.at[0], sp)
    v_x = (space_peer, 16, lambda p: send_v.at[p], recv_v, s_in.at[1], r_in.at[1], sp)
    c_x = (space_peer, 16, lambda p: send_c.at[p], recv_c, s_in.at[2], r_in.at[2], sp)
    start_all(*kq_x)
    own_to_sibling = copy(kv.at[tm], kv.at[tm], s_sib, r_sib, (dp, sibling, sp))
    own_to_sibling.start()
    gap = jnp.zeros((8, TOK), F32)

    def pack(src, dst):
        @pl.loop(0, HEADS)
        def _(h):
            dst[h] = jnp.concatenate([src[head_rows(h), :], gap], axis=0).astype(BF16)

    transpose_in(value_s, t0)
    pack(t0, send_v)
    start_all(*v_x)
    transpose_in(cot, cott)
    pack(cott, send_c)
    recv_kq[sp] = send_kq[sp]
    recv_v[sp] = send_v[sp]
    recv_c[sp] = send_c[sp]
    codes_all[sp] = codes_own[...]
    for i in range(D // 128):
        xt[pl.ds(i * 128, 128), :] = patches[:, pl.ds(i * 128, 128)].astype(F32).T
    transpose_in(query_t, qtt)
    loads[id(bm)].wait()
    for src, dst in ((at, ah), (bm, bh)):
        for i in range(D // 128):
            abt[pl.ds(i * 128, 128), :] = src[:, pl.ds(i * 128, 128)].astype(F32).T
        dst[...] = abt[head_rows(sp), :].T.astype(BF16)

    received_all(*codes_x)
    received_all(*kq_x)
    received_all(*v_x)

    @pl.loop(0, 8)
    def _(j):
        lanes = pl.ds(pl.multiple_of(j * 128, 128), 128)
        even, odd = 2 * j, 2 * j + 1
        kq = to_frames(recv_kq[even].astype(F32), recv_kq[odd].astype(F32))
        value = to_frames(recv_v[even].astype(F32), recv_v[odd].astype(F32))
        codes = to_frames(codes_all[even].astype(F32), codes_all[odd].astype(F32))
        for f in range(2):
            code = codes[f].astype(BF16)
            cc[f, :, lanes] = code
            keys = kq[f][:HEAD_DIM]
            query = kq[f][HEAD_DIM:] + dot(bh[pl.ds(0, 16), :], code[:16], TN)
            values = rounded(value[f][:HEAD_DIM] + dot(bh[pl.ds(16, 16), :], code[16:], TN))
            kt[f, :, lanes] = keys.astype(BF16)
            kn[f, lanes, :] = keys.T.astype(BF16)
            qt[f, :, lanes] = query.astype(BF16)
            vt[f, :, lanes] = values.astype(BF16)
            vn[f, lanes, :] = values.T.astype(BF16)

    def forward(f):
        @pl.loop(0, LENGTH // CHUNK)
        def _(i):
            lanes = pl.ds(pl.multiple_of(i * CHUNK, CHUNK), CHUNK)
            scores = dot(kn[f], qt[f, :, lanes])
            weights = jnp.exp2((scores - jnp.max(scores, axis=0, keepdims=True)) * (SCALE * LOG2E))
            p = weights * (1.0 / jnp.sum(weights, axis=0, keepdims=True))
            low = p.astype(BF16)
            probs[f, :, lanes] = p * SCALE
            probs_low[f, :, lanes] = low
            out = dot(vt[f], low)
            ot[f, :, lanes] = out
            oe[f, :, lanes] = out + dot(vt[f], (p - low.astype(F32)).astype(BF16))

    forward(0)
    forward(1)

    @pl.loop(0, 8)
    def _(j):
        lanes = pl.ds(pl.multiple_of(j * 128, 128), 128)
        pair = from_frames(ot[0, :, lanes], ot[1, :, lanes])
        for k in range(2):
            o_send[2 * j + k] = jnp.concatenate([pair[k], jnp.zeros((8, TOK), F32)], axis=0).astype(BF16)

    o_x = (space_peer, 16, lambda p: o_send.at[p], o_recv, s_o, r_o, sp)
    start_all(*o_x)
    o_recv[sp] = o_send[sp]
    sent_all(*codes_x)
    sent_all(*kq_x)
    sent_all(*v_x)
    received_all(*o_x)
    start_all(*c_x)

    @pl.loop(0, HEADS)
    def _(h):
        rows = head_rows(h)
        ht[rows, :] = rounded(xt[rows, :] + o_recv[h].astype(F32)[:HEAD_DIM])

    hidden = ht[...].astype(BF16)
    codes_t = dot(at[pl.ds(32, 32), :], hidden).astype(BF16)
    codes_tq = codes_t[:16]
    ctv[tm] = codes_t[16:]
    ctv_x = (tm_peer, 4, lambda p: ctv.at[tm], ctv, s_ctv, r_ctv, tm)
    start_all(*ctv_x)
    sent_all(*o_x)
    qtt[...] = rounded(qtt[...] + dot(bm[pl.ds(32, 16), :], codes_tq, TN))
    received_all(*ctv_x)
    for s in range(SOURCES):
        lv[s] = dot(bm[pl.ds(48, 16), :], ctv[s], TN)

    def temporal_head(h):
        rows = head_rows(h)
        q, g = qtt[rows, :], cott[rows, :]
        keys, values, straight, turned, d_straight, d_turned = [], [], [], [], [], []
        for s in range(SOURCES):
            both = kv[s, h].astype(F32)
            k, v = both[:HEAD_DIM], rounded(both[HEAD_DIM:] + lv[s, rows, :])
            k_r, v_r = half_turn(k), half_turn(v)
            keys.append((k, k_r))
            values.append((v, v_r))
            straight.append(jnp.sum(q * k, axis=0, keepdims=True))
            turned.append(jnp.sum(q * k_r, axis=0, keepdims=True))
            d_straight.append(jnp.sum(g * v, axis=0, keepdims=True))
            d_turned.append(jnp.sum(g * v_r, axis=0, keepdims=True))
        scores = jnp.concatenate(straight + turned, axis=0)
        weights = jnp.exp2((scores - jnp.max(scores, axis=0, keepdims=True)) * (SCALE * LOG2E))
        p = weights * (1.0 / jnp.sum(weights, axis=0, keepdims=True))
        dprob = jnp.concatenate(d_straight + d_turned, axis=0)
        inner = jnp.sum(p * dprob, axis=0, keepdims=True)
        dscore = rounded(p * (dprob - inner) * SCALE)
        low = rounded(p)
        low_r, g_r = half_turn(low), half_turn(g)
        out = jnp.zeros((HEAD_DIM, TOK), F32)
        dquery = jnp.zeros((HEAD_DIM, TOK), F32)
        for s in range(SOURCES):
            out = out + low[s : s + 1] * values[s][0] + low[s + 4 : s + 5] * values[s][1]
            dquery = dquery + dscore[s : s + 1] * keys[s][0] + dscore[s + 4 : s + 5] * keys[s][1]
            dq5[1 + s, rows, :] = low[s : s + 1] * g + low_r[s + 4 : s + 5] * g_r
        dq5[0, rows, :] = dquery
        t0[rows, :] = ht[rows, :] + rounded(out)

    own_to_sibling.wait_recv()

    def relay_chunk(c):
        copy(z_slot(tm, c), z_slot(across, c), s_z, r_z.at[c], (dp, across, sp)).wait_recv()
        copy(z_slot(across, c), z_slot(across, c), s_fwd, r_fwd.at[c], (dp, sibling, sp)).start()

    sent_all(*c_x)
    received_all(*c_x)

    @pl.loop(0, 8)
    def _(j):
        lanes = pl.ds(pl.multiple_of(j * 128, 128), 128)
        even, odd = 2 * j, 2 * j + 1
        grad = to_frames(recv_c[even].astype(F32), recv_c[odd].astype(F32))
        for f in range(2):
            cf[f, :, lanes] = grad[f][:HEAD_DIM]

    relay_chunk(0)
    for c in range(ZCHUNKS):
        if c + 1 < ZCHUNKS:
            relay_chunk(c + 1)
        copy(z_slot(across, c), z_slot(far, c), s_fwd, r_fwd.at[c], (dp, sibling, sp)).wait_recv()

        @pl.loop(c * ZHEADS, (c + 1) * ZHEADS)
        def _(h):
            temporal_head(h)

    for s in range(SOURCES):
        dcv_own[s] = dot(bm[pl.ds(48, 16), :], dq5[1 + s].astype(BF16)).astype(BF16)
    dcv_x = (tm_peer, 4, lambda p: dcv_own.at[p], dcv, s_dcv, r_dcv, tm)
    start_all(*dcv_x)
    sent_all(*ctv_x)
    dcv[tm] = dcv_own[tm]
    dq_t = dq5[0].astype(BF16)
    dcodes_tq = dot(bm[pl.ds(32, 16), :], dq_t)
    grad_b = [dot(codes_tq, dq_t, NT)]
    part_v = dot(ctv[0], dq5[1].astype(BF16), NT)
    for s in range(1, SOURCES):
        part_v = part_v + dot(ctv[s], dq5[1 + s].astype(BF16), NT)
    grad_b.append(part_v)
    copy(kv.at[tm], kv.at[tm], s_z, r_z.at[0], (dp, across, sp)).wait_send()
    own_to_sibling.wait_send()
    copy(kv.at[across], kv.at[across], s_fwd, r_fwd.at[0], (dp, sibling, sp)).wait_send()
    received_all(*dcv_x)
    dcodes_tv = sum_slots(dcv, SOURCES)
    dcodes_t = jnp.concatenate([dcodes_tq, dcodes_tv], axis=0).astype(BF16)
    dct_own[...] = dcodes_t
    dct_x = (space_peer, 16, lambda p: dct_own, dct_all, s_dct, r_dct, sp)
    start_all(*dct_x)
    dct_all[sp] = dcodes_t

    grad_a = dot(dcodes_t, ht[...].astype(BF16), NT)
    halves = [grad_a, jnp.concatenate(grad_b, axis=0)]
    for r in range(2):
        for c in range(9):
            gt_send[9 * r + c] = halves[r][:, 128 * c : 128 * (c + 1)].astype(BF16)
    gt_x = (block_peer, 32, lambda p: gt_send.at[p], gt_recv, s_gt, r_gt, block, PIECES)
    start_all(*gt_x)

    for i in range(D // 128):
        cols = pl.ds(i * 128, 128)
        mixed[:, cols] = t0[cols, :].T.astype(BF16)

    sent_all(*dcv_x)
    received_all(*dct_x)

    @pl.loop(0, 8)
    def _(j):
        lanes = pl.ds(pl.multiple_of(j * 128, 128), 128)
        even, odd = 2 * j, 2 * j + 1
        codes = to_frames(dct_all[even].astype(F32), dct_all[odd].astype(F32))
        for f in range(2):
            gf[f, :, lanes] = (
                cf[f, :, lanes] + dot(ah[pl.ds(32, 32), :], codes[f].astype(BF16), TN)
            ).astype(BF16)

    dv[...] = jnp.zeros_like(dv)

    def backward(f):
        @pl.loop(0, LENGTH // CHUNK)
        def _(i):
            lanes = pl.ds(pl.multiple_of(i * CHUNK, CHUNK), CHUNK)
            g = gf[f, :, lanes]
            inner = jnp.sum(g.astype(F32) * oe[f, :, lanes], axis=0, keepdims=True)
            dprob = dot(vn[f], g)
            dscore = (probs[f, :, lanes] * (dprob - inner)).astype(BF16)
            dq[f, :, lanes] = dot(kt[f], dscore)
            dv[f] += dot(g, probs_low[f, :, lanes], NT)

    backward(0)
    z_t_x = (z_peer, 16, lambda p: z_t.at[z], z_t, s_zt, r_zt, z)

    @pl.when(block < PIECES)
    def _():
        gt_recv[block] = gt_send[block]
        received_all(block_peer, 32, lambda p: gt_send.at[p], gt_recv, s_gt, r_gt, block)
        z_t[z] = sum_slots(gt_recv, 32).astype(BF16)
        start_all(*z_t_x)

    backward(1)
    pad = jnp.zeros((128 - HEAD_DIM, LENGTH), F32)
    gb_q = jnp.zeros((16, 128), F32)
    gb_v = jnp.zeros((16, 128), F32)
    for f in range(2):
        dctf[f, pl.ds(0, 16), :] = dot(bh[pl.ds(0, 16), :], dq[f].astype(BF16))
        dctf[f, pl.ds(16, 16), :] = dot(bh[pl.ds(16, 16), :], dv[f].astype(BF16))

    @pl.loop(0, 8)
    def _(j):
        lanes = pl.ds(pl.multiple_of(j * 128, 128), 128)
        pair = from_frames(dctf[0, :, lanes], dctf[1, :, lanes])
        dcs_send[2 * j] = pair[0].astype(BF16)
        dcs_send[2 * j + 1] = pair[1].astype(BF16)

    dcs_x = (space_peer, 16, lambda p: dcs_send.at[p], dcs_recv, s_dcs, r_dcs, sp)
    start_all(*dcs_x)
    dcs_recv[sp] = dcs_send[sp]
    for f in range(2):
        dq_f = jnp.concatenate([dq[f], pad], axis=0).astype(BF16)
        dv_f = jnp.concatenate([dv[f], pad], axis=0).astype(BF16)
        gb_q = gb_q + dot(cc[f, pl.ds(0, 16), :], dq_f, NT)
        gb_v = gb_v + dot(cc[f, pl.ds(16, 16), :], dv_f, NT)
    gb_send[0] = gb_q.astype(BF16)
    gb_send[1] = gb_v.astype(BF16)
    to_sibling = copy(gb_send.at[1 - core], gb_recv, s_gb, r_gb, (dp, sibling, sp))
    to_sibling.start()
    sent_all(*dct_x)
    sent_all(*gt_x)
    received_all(*dcs_x)
    dcodes_s = sum_slots(dcs_recv, 16).astype(BF16)
    grad_s = dot(dcodes_s, patches[...])
    for r in range(2):
        for c in range(9):
            gs_send[9 * r + c] = grad_s[16 * r : 16 * (r + 1), 128 * c : 128 * (c + 1)].astype(BF16)
    gs_x = (block_peer, 32, lambda p: gs_send.at[p], gs_recv, s_gs, r_gs, block, PIECES)
    start_all(*gs_x)
    sent_all(*dcs_x)
    to_sibling.wait_recv()
    z_s[z, pl.ds(16, 16), :] = (gb_send[core].astype(F32) + gb_recv[...].astype(F32)).astype(BF16)

    @pl.when(block < PIECES)
    def _():
        received_all(*z_t_x)
        ag_t[block] = sum_slots(z_t, 16).astype(BF16)
        gs_recv[block] = gs_send[block]
        received_all(block_peer, 32, lambda p: gs_send.at[p], gs_recv, s_gs, r_gs, block)
        z_s[z, pl.ds(0, 16), :] = sum_slots(gs_recv, 32).astype(BF16)

    z_half = z_s.at[pl.ds(0, 16), pl.ds(16, 16)]
    z_s_x = (z_peer, 16, lambda p: z_s.at[z], z_s, s_zs, r_zs, z)
    z_h_x = (z_peer, 16, lambda p: z_half.at[z], z_half, s_zs, r_zs, z)
    has_piece = pl.when(block < PIECES)
    no_piece = pl.when(block >= PIECES)
    has_piece(lambda: start_all(*z_s_x))
    no_piece(lambda: start_all(*z_h_x))
    ag_t_x = (block_peer, 32, lambda p: ag_t.at[block], ag_t, s_agt, r_agt, block)

    @pl.when(block < PIECES)
    def _():
        start_all(*ag_t_x)
        sent_all(*z_t_x)

    sent_all(*gs_x)
    to_sibling.wait_send()
    received_all(*ag_t_x, PIECES)
    for piece in range(PIECES):
        out = (ga, gb)[piece // 9]
        out[pl.ds(32, 32), pl.ds(128 * (piece % 9), 128)] = ag_t[piece]

    @pl.when(block < PIECES)
    def _():
        sent_all(*ag_t_x)

    ag_half = ag_s.at[pl.ds(0, 32), pl.ds(16, 16)]
    ag_s_x = (block_peer, 32, lambda p: ag_s.at[block], ag_s, s_ags, r_ags, block)
    ag_h_x = (block_peer, 32, lambda p: ag_half.at[block], ag_half, s_ags, r_agh, block)

    @has_piece
    def _():
        received_all(*z_s_x)
        ag_s[block] = sum_slots(z_s, 16).astype(BF16)
        start_all(*ag_s_x)
        sent_all(*z_s_x)
        received_all(*ag_s_x, PIECES)
        everything = ag_half.at[pl.ds(0, 32 - PIECES)]
        copy(everything, everything, s_ags, r_agh, (dp, sibling, sp)).wait_recv()

    @no_piece
    def _():
        received_all(*z_h_x)
        total = z_s[0, pl.ds(16, 16), :].astype(F32)
        for k in range(1, 16):
            total = total + z_s[k, pl.ds(16, 16), :].astype(F32)
        ag_s[block, pl.ds(16, 16), :] = total.astype(BF16)
        start_all(*ag_h_x)
        sent_all(*z_h_x)
        received_all(*ag_s_x, PIECES)
        others = ag_half.at[pl.ds(0, 31 - PIECES)]
        copy(others, others, s_ags, r_agh, (dp, sibling, sp)).wait_recv()

    for piece in range(PIECES):
        rows = pl.ds(16 * (piece // 9), 16)
        ga[rows, pl.ds(128 * (piece % 9), 128)] = ag_s[piece, pl.ds(0, 16), :]
    for r in range(2):
        tiles = [jnp.zeros((16, 128), F32) for _ in range(D // 128)]
        for h in range(HEADS):
            first, offset = divmod(h * HEAD_DIM, 128)
            piece = ag_s[16 * r + h, pl.ds(16, 16), :].astype(F32)
            if offset:
                piece = pltpu.roll(piece, offset, 1)
            lane = lax.broadcasted_iota(jnp.int32, (1, 128), 1)
            tiles[first] = tiles[first] + jnp.where(lane >= offset, piece, 0.0)
            if offset + HEAD_DIM > 128:
                tiles[first + 1] = tiles[first + 1] + jnp.where(lane < offset, piece, 0.0)
        for i in range(D // 128):
            gb[pl.ds(16 * r, 16), pl.ds(128 * i, 128)] = tiles[i].astype(BF16)
    has_piece(lambda: sent_all(*ag_s_x))
    no_piece(lambda: sent_all(*ag_h_x))


def scratch():
    def f32(*shape):
        return pltpu.VMEM(shape, F32)

    def bf16(*shape):
        return pltpu.VMEM(shape, BF16)

    def sems(*shape):
        return pltpu.SemaphoreType.DMA(shape)

    whole = f32(D, TOK)
    one = pltpu.SemaphoreType.DMA
    return [
        *[bf16(TOK, D)] * 8, bf16(64, D), bf16(64, D), sems(10),
        bf16(64, HEAD_DIM), bf16(64, HEAD_DIM), f32(D, 64),
        whole, whole, whole, whole, whole, whole, f32(SOURCES, D, TOK), f32(1 + SOURCES, D, TOK),
        bf16(HEADS, 144, TOK), bf16(HEADS, 144, TOK), bf16(HEADS, 80, TOK), bf16(HEADS, 80, TOK),
        bf16(HEADS, 80, TOK), bf16(HEADS, 80, TOK), bf16(HEADS, 32, TOK), bf16(32, TOK),
        bf16(2, HEAD_DIM, LENGTH), bf16(2, LENGTH, HEAD_DIM), bf16(2, HEAD_DIM, LENGTH), bf16(2, LENGTH, HEAD_DIM),
        bf16(2, HEAD_DIM, LENGTH), f32(2, HEAD_DIM, LENGTH), bf16(2, 32, LENGTH), f32(2, LENGTH, LENGTH),
        bf16(2, LENGTH, LENGTH), f32(2, HEAD_DIM, LENGTH), f32(2, HEAD_DIM, LENGTH),
        bf16(HEADS, 80, TOK), bf16(HEADS, 80, TOK),
        bf16(SOURCES, HEADS, 144, TOK), bf16(SOURCES, 16, TOK), bf16(SOURCES, 16, TOK), bf16(SOURCES, 16, TOK),
        bf16(32, TOK), bf16(HEADS, 32, TOK), f32(2, 32, LENGTH), bf16(2, HEAD_DIM, LENGTH),
        f32(2, HEAD_DIM, LENGTH), f32(2, HEAD_DIM, LENGTH), bf16(HEADS, 32, TOK), bf16(HEADS, 32, TOK),
        bf16(PIECES, 32, 128), bf16(32, 32, 128), bf16(16, 32, 128), bf16(32, 32, 128),
        bf16(PIECES, 16, 128), bf16(32, 16, 128), bf16(2, 16, 128), bf16(16, 128), bf16(16, 32, 128), bf16(32, 32, 128),
        sems(3), sems(3), one, one, one, one,
        one, sems(ZCHUNKS), one, one, one, sems(ZCHUNKS),
        one, one, one, one, one, one, one, one,
        one, one, one, one, one, one,
        one, one, one, one, one, one, one, one, one,
    ]


def hand_over(mixed, ga, gb, mixed_out, ga_out, gb_out):
    mixed_out[...] = mixed[...]
    ga_out[...] = ga[...].astype(F32) * FACTOR
    gb_out[...] = gb[...].astype(F32) * FACTOR


def per_device(
    patches, query_s, key_s, value_s, query_t, key_t, value_t, adapters_a, adapters_b, cotangent
):
    at = jnp.swapaxes(adapters_a, 1, 2).reshape(64, D)
    bm = adapters_b.reshape(64, D)
    tokens = [
        array.reshape(TOK, D)
        for array in (patches, query_s, key_s, value_s, query_t, key_t, value_t, cotangent)
    ]
    out_shape = (
        jax.ShapeDtypeStruct((TOK, D), BF16),
        jax.ShapeDtypeStruct((64, D), F32),
        jax.ShapeDtypeStruct((64, D), F32),
    )
    results = pl.pallas_call(
        kernel,
        out_shape=(
            jax.ShapeDtypeStruct((TOK, D), BF16),
            jax.ShapeDtypeStruct((64, D), BF16),
            jax.ShapeDtypeStruct((64, D), BF16),
        ),
        in_specs=[pl.BlockSpec(memory_space=pl.ANY)] * 10,
        out_specs=[pl.BlockSpec(memory_space=pltpu.VMEM)] * 3,
        scratch_shapes=scratch(),
        compiler_params=pltpu.CompilerParams(
            collective_id=0, has_side_effects=True, vmem_limit_bytes=56 * 1024 * 1024
        ),
    )(*tokens, at, bm)
    mixed, ga, gb = pl.pallas_call(
        hand_over,
        out_shape=out_shape,
        in_specs=[pl.BlockSpec(memory_space=pltpu.VMEM)] * 3,
        out_specs=[pl.BlockSpec(memory_space=pltpu.VMEM)] * 3,
    )(*results)
    grads_a = jnp.swapaxes(ga.reshape(4, 16, D), 1, 2)
    grads_b = gb.reshape(4, 16, D)
    return mixed.reshape(patches.shape), grads_a, grads_b


def solution(mesh):
    tokens = P("dp", "tm", "space", None)
    return jax.shard_map(
        per_device,
        mesh=mesh,
        in_specs=(tokens,) * 7 + (P(), P(), tokens),
        out_specs=(tokens, P(), P()),
        check_vma=False,
    )
```
